32 devices in a mesh: groups: 2 (over x), dp: 16 (over z, y, core).
Axes of the slice: x: 2, y: 2, z: 4, core: 2. Of those that a mesh axis runs over, the one named last changes fastest.
Arguments:
- train_hidden: bfloat16 [128, 40, 14336], P(('groups', 'dp')), parts along dimension 0, may hold values from -6 to 6
- train_cot: bfloat16 [128, 40, 4096], P(('groups', 'dp')), parts along dimension 0, may hold values from -6 to 6
- query_hidden: bfloat16 [192, 16, 14336], P(('groups', 'dp')), parts along dimension 0, may hold values from -6 to 6
- query_cot: bfloat16 [192, 16, 4096], P(('groups', 'dp')), parts along dimension 0, may hold values from -6 to 6
- proj_in: bfloat16 [64, 14336], replicated, may hold values from -0.046875 to 0.046875
- proj_out: bfloat16 [64, 4096], replicated, may hold values from -0.09375 to 0.09375
- hess_inv: float32 [8192, 4096], P(('groups', 'dp')), parts along dimension 0, as said below
Outputs:
- scores: float32 [128, 96], P(('groups', 'dp')), parts along dimension 0
The draws below stay inside these ranges and needn't reach their ends.
There are 2 independent parts, one for each index of `groups`. The reference program is written for one: setup_inputs(seed, part) draws one part's arguments, and reference() takes and returns one part's arrays. A program takes and returns all parts, laid end to end along the dimension named above; an argument that names none is the same for every part. Nothing has to cross between parts.
Inputs may be any that keep to these rules, and one draw needn't show every extreme that they name: hess_inv is symmetric and positive definite.
All inputs are finite; a program needn't handle non-finite values.
Results may differ from the reference program's by a relative error of at most 0.0075.
Values may be sent and summed in bfloat16 or wider, within the bound.
No kernel may reach another device: no remote copies, remote signals or barrier semaphores. Data moves between devices by JAX's collectives and lax.ppermute only.
A program may use at most 64 MiB of HBM per device.

```python
import math
import jax
import jax.numpy as jnp
from jax import lax

D = 4096
FF = 14336
R = 64
SEQ_LEN = 40
QLEN = 16
K = 4096
TRAIN = 64
QUERIES = 96


def draw_hess_inv(key, part):
    key = jax.random.fold_in(key, 11)
    first, second = jax.random.split(key, 2)
    spread = 0.85 / math.sqrt(K)
    entries = jax.random.uniform(first, (K, K), jnp.float32, -spread, spread)
    symmetric = (entries + entries.T) * 0.5
    position = jnp.arange(K, dtype=jnp.float32) / K
    diagonal = (1.2 + 1.2 * jax.random.uniform(second, (K,), jnp.float32)) * (1.0 + 2.0 * position)
    rows_index = jnp.arange(K)[:, None]
    cols_index = jnp.arange(K)[None, :]
    matrix = jnp.where(rows_index == cols_index, diagonal[:, None], symmetric)
    return matrix


def levels(stream_key, shape, cuts, smallest, top_value):
    factor_of, own = 1.0, jax.random.fold_in(stream_key, 6)
    for dim, blocks in cuts:
        heights = jnp.exp(jax.random.uniform(jax.random.fold_in(own, dim), (blocks,), jnp.float32, smallest / len(cuts), top_value / len(cuts)))
        factor_of = factor_of * jnp.repeat(heights, shape[dim] // blocks).reshape([-1 if axis == dim else 1 for axis in range(len(shape))])
    return factor_of


def normal_values(rng, shape, scale, bound, cuts=(), kind=jnp.bfloat16):
    array = jax.random.normal(rng, shape, jnp.float32) * scale
    if len(cuts) > 0:
        array = levels(rng, shape, cuts, -0.22, 0.18) * array
    return jnp.clip(array, min=-bound, max=bound).astype(kind)


def setup_inputs(seed: int = 0, part: int = 0) -> dict:
    keys = jax.random.split(jax.random.key(seed), 8)
    own_keys = jax.random.split(jax.random.fold_in(keys[7], part), 8)
    train_hidden = normal_values(own_keys[0], (TRAIN, SEQ_LEN, FF), 1.0, 6.0, ((0, 16),))
    train_cot = normal_values(own_keys[1], (TRAIN, SEQ_LEN, D), 1.0, 6.0, ((0, 16),))
    query_hidden = normal_values(own_keys[2], (QUERIES, QLEN, FF), 1.0, 6.0, ((0, 16),))
    query_cot = normal_values(own_keys[3], (QUERIES, QLEN, D), 1.0, 6.0, ((0, 16),))
    proj_in = normal_values(keys[4], (R, FF), FF ** -0.5, 0.046875)
    proj_out = normal_values(keys[5], (R, D), D ** -0.5, 0.09375)
    hess_inv = draw_hess_inv(jax.random.fold_in(jax.random.fold_in(keys[7], part), 71), part)
    return dict(train_hidden=train_hidden, train_cot=train_cot, query_hidden=query_hidden, query_cot=query_cot, proj_in=proj_in, proj_out=proj_out, hess_inv=hess_inv)


def example_grads(hidden, cotangent, proj_in, proj_out):
    number, length, inner = hidden.shape
    outer_width = cotangent.shape[2]
    rank = proj_in.shape[0]
    inputs = jnp.dot(hidden.reshape(number * length, inner), proj_in.T, preferred_element_type=jnp.float32).astype(jnp.bfloat16)
    outputs = jnp.dot(cotangent.reshape(number * length, outer_width), proj_out.T, preferred_element_type=jnp.float32).astype(jnp.bfloat16)
    inputs = inputs.reshape(number, length, rank).astype(jnp.float32)
    outputs = outputs.reshape(number, length, rank).astype(jnp.float32)
    summed = jnp.einsum('sto,sti->soi', outputs, inputs) * (1.0 / length)
    return summed.astype(jnp.bfloat16).reshape(number, rank * rank)

def reference(train_hidden, train_cot, query_hidden, query_cot, proj_in, proj_out, hess_inv):
    train_grads = example_grads(train_hidden, train_cot, proj_in, proj_out)
    query_grads = example_grads(query_hidden, query_cot, proj_in, proj_out)
    precond = jnp.dot(query_grads.astype(jnp.float32), hess_inv, precision=lax.Precision.HIGHEST)
    precond_bf = precond.astype(jnp.bfloat16)
    self_inf = lax.optimization_barrier(jnp.sum(query_grads.astype(jnp.float32) * precond_bf.astype(jnp.float32), axis=1))
    raw = jnp.dot(train_grads, precond_bf.T, preferred_element_type=jnp.float32)
    return raw / jnp.sqrt(self_inf)[None, :]
```

```python
import functools

import jax
import jax.numpy as jnp
from jax import lax
from jax.experimental import pallas as pl
from jax.experimental.pallas import tpu as pltpu
from jax.sharding import PartitionSpec as P

F32, BF16 = jnp.float32, jnp.bfloat16
NT = (((1,), (1,)), ((), ()))
VMEM = pl.BlockSpec(memory_space=pltpu.VMEM)
HBM = pl.BlockSpec(memory_space=pltpu.HBM)
INNER = 4
GROUP = 256


def dot(a, b):
    return jnp.dot(a, b, preferred_element_type=F32)


def dot_nt(a, b):
    return lax.dot_general(a, b, NT, preferred_element_type=F32)


def in_hbm(x):
    return pltpu.with_memory_space_constraint(x, pltpu.HBM)


def iota(shape, dim):
    return lax.broadcasted_iota(jnp.int32, shape, dim)


def example_grads(hidden, cotangent, proj_in, proj_out):
    number, length, inner = hidden.shape
    outer_width = cotangent.shape[2]
    rank = proj_in.shape[0]
    inputs = jnp.dot(
        hidden.reshape(number * length, inner), proj_in.T, preferred_element_type=jnp.float32
    ).astype(jnp.bfloat16)
    outputs = jnp.dot(
        cotangent.reshape(number * length, outer_width),
        proj_out.T,
        preferred_element_type=jnp.float32,
    ).astype(jnp.bfloat16)
    inputs = inputs.reshape(number, length, rank)
    outputs = outputs.reshape(number, length, rank)
    summed = jnp.einsum("sto,sti->soi", outputs, inputs, preferred_element_type=jnp.float32) * (
        1.0 / length
    )
    return summed.astype(jnp.bfloat16).reshape(number, rank * rank)


def general(train_hidden, train_cot, query_hidden, query_cot, proj_in, proj_out, hess_inv):
    train_grads = example_grads(train_hidden, train_cot, proj_in, proj_out)
    query_grads = example_grads(query_hidden, query_cot, proj_in, proj_out)
    full_query = lax.all_gather(query_grads, "dp", axis=0, tiled=True).astype(jnp.float32)
    product = jnp.dot(full_query, hess_inv.T, precision=lax.Precision.HIGHEST)
    full_precond = lax.all_gather(product.astype(jnp.bfloat16), "dp", axis=1, tiled=True)
    self_inf = jnp.sum(full_query * full_precond.astype(jnp.float32), axis=1)
    raw = jnp.dot(train_grads, full_precond.T, preferred_element_type=jnp.float32)
    return raw / jnp.sqrt(self_inf)[None, :]


def project_kernel(
    planes, number, length, chunks, me_ref, th_ref, tc_ref, qh_ref, qc_ref, pi_ref, po_ref, *rest
):
    outs, (th, tc, qh, qc, pi, po, grads, sems) = rest[:planes], rest[planes:]
    inner = th.shape[1]
    width = inner // chunks
    rank = pi.shape[0]
    tokens = th.shape[0]
    queries = qh.shape[0]

    copies = {}

    def load(name, src, dst, part=None):
        if part is not None:
            cols = pl.ds(part * width, width)
            src, dst = src.at[:, cols], dst.at[:, cols]
        copies[name, part] = pltpu.make_async_copy(src, dst, sems.at[len(copies)])
        copies[name, part].start()

    load("po", po_ref, po)
    load("tc", tc_ref, tc)
    load("qc", qc_ref, qc)
    for c in range(chunks):
        load("pi", pi_ref, pi, c)
        load("th", th_ref, th, c)
        load("qh", qh_ref, qh, c)

    rows = rank // 2 * number
    copies["po", None].wait()
    copies["tc", None].wait()
    t_out = dot_nt(po[...], tc[...]).astype(BF16)
    row, col = iota((rows, tokens), 0), iota((rows, tokens), 1)
    own = row % number == col // length
    lefts = []
    for half in range(2):
        pick = iota((rows, rank), 1) == 2 * (iota((rows, rank), 0) // number) + half
        lefts.append(jnp.where(own, dot(pick.astype(BF16), t_out), 0.0).astype(BF16))
    copies["qc", None].wait()
    q_out = dot_nt(qc[...], po[...])

    t_in = jnp.zeros((tokens, rank), F32)
    q_in = jnp.zeros((queries, rank), F32)
    for c in range(chunks):
        cols = slice(c * width, (c + 1) * width)
        copies["pi", c].wait()
        copies["th", c].wait()
        t_in += dot_nt(th[:, cols], pi[:, cols])
        copies["qh", c].wait()
        q_in += dot_nt(qh[:, cols], pi[:, cols])

    spread = jnp.concatenate([t_in, t_in], axis=1).astype(BF16)
    lane = iota((tokens, 2 * rank), 1)
    total = jnp.zeros((rows, 2 * rank), F32)
    for half in range(2):
        right = jnp.where(lane // rank == half, spread, jnp.zeros_like(spread))
        total += dot(lefts[half], right)
    grads[...] = (total * (1.0 / length)).astype(BF16)
    message = jnp.concatenate([q_in, q_out], axis=1).astype(BF16)

    plane = me_ref[0] // INNER
    share = rows // planes
    for k in range(planes):
        outs[k][:queries, :] = message
        start = pl.multiple_of((plane ^ k) * share, share)
        outs[k][queries:, :] = grads[pl.ds(start, share), :]


def project(me, planes, train_hidden, train_cot, query_hidden, query_cot, proj_in, proj_out):
    number, length, inner = train_hidden.shape
    width = train_cot.shape[2]
    rank = proj_in.shape[0]
    tokens, queries = number * length, query_hidden.shape[0] * query_hidden.shape[1]
    rows = rank // 2 * number
    chunks = 4
    out = pltpu.VMEM((queries + rows // planes, 2 * rank), BF16)
    return pl.pallas_call(
        functools.partial(project_kernel, planes, number, length, chunks),
        out_shape=[out] * planes,
        in_specs=[pl.BlockSpec(memory_space=pltpu.SMEM)] + [HBM] * 6,
        out_specs=[VMEM] * planes,
        scratch_shapes=[
            pltpu.VMEM((tokens, inner), BF16),
            pltpu.VMEM((tokens, width), BF16),
            pltpu.VMEM((queries, inner), BF16),
            pltpu.VMEM((queries, width), BF16),
            pltpu.VMEM((rank, inner), BF16),
            pltpu.VMEM((rank, width), BF16),
            pltpu.VMEM((rows, 2 * rank), BF16),
            pltpu.SemaphoreType.DMA((3 * chunks + 3,)),
        ],
        compiler_params=pltpu.CompilerParams(vmem_limit_bytes=20 * 2**20),
        name="project",
    )(
        me,
        in_hbm(train_hidden.reshape(tokens, inner)),
        in_hbm(train_cot.reshape(tokens, width)),
        in_hbm(query_hidden.reshape(queries, inner)),
        in_hbm(query_cot.reshape(queries, width)),
        in_hbm(proj_in),
        in_hbm(proj_out),
    )


def split_kernel(chunks, hess_ref, after_ref, high_ref, low_ref, hess, sems):
    width = hess.shape[1] // chunks
    copies = []
    for c in range(chunks):
        cols = pl.ds(c * width, width)
        copies.append(pltpu.make_async_copy(hess_ref.at[:, cols], hess.at[:, cols], sems.at[c]))
        copies[-1].start()
    for c in range(chunks):
        copies[c].wait()
        cols = slice(c * width, (c + 1) * width)
        h = hess[:, cols]
        high = h.astype(BF16)
        high_ref[:, cols] = high
        low_ref[:, cols] = (h - high.astype(F32)).astype(BF16)


def split(hess_inv, after):
    chunks = 4
    out = pltpu.VMEM(hess_inv.shape, BF16)
    return pl.pallas_call(
        functools.partial(split_kernel, chunks),
        out_shape=[out] * 2,
        in_specs=[HBM, VMEM],
        out_specs=[VMEM] * 2,
        scratch_shapes=[
            pltpu.VMEM(hess_inv.shape, F32),
            pltpu.SemaphoreType.DMA((chunks,)),
        ],
        compiler_params=pltpu.CompilerParams(vmem_limit_bytes=20 * 2**20),
        cost_estimate=pl.CostEstimate(
            flops=3 * hess_inv.size, bytes_accessed=8 * hess_inv.size, transcendentals=0
        ),
        name="split",
    )(in_hbm(hess_inv), after)


def score_kernel(n, number, qlen, slots, me_ref, *rest):
    pieces, (high_ref, low_ref, out_ref, tok, train, grads) = rest[:-6], rest[-6:]
    me = me_ref[0]
    block, coords = high_ref.shape
    lanes = tok.shape[1]
    rank = lanes // 2
    tokens = tok.shape[0] // n
    pairs = rank // 2
    local = block // lanes
    tile = local * number
    mine = me % INNER

    slots = iter(slots)
    for piece in pieces:
        for part in range(piece.shape[0]):
            source = me ^ next(slots)
            start = pl.multiple_of(source * tokens, tokens)
            tok[pl.ds(start, tokens), :] = piece[part, :tokens, :]
            share = piece[part, tokens:, :].astype(F32)
            picked = share[:tile]
            for j in range(1, INNER):
                picked = jnp.where(mine == j, share[j * tile : (j + 1) * tile], picked)
            train[source] = picked

    group = GROUP
    per = group // qlen
    pick = (iota((rank, lanes), 1) == iota((rank, lanes), 0) + rank).astype(BF16)
    shift = (iota((lanes, lanes), 1) == iota((lanes, lanes), 0) + rank).astype(BF16)
    own = (iota((per, group), 1) // qlen == iota((per, group), 0)).astype(BF16)
    low = iota((group, lanes), 1) < rank
    for g in range(n * tokens // group):
        x = tok[g * group : (g + 1) * group, :]
        outs = dot_nt(pick, x)
        right = jnp.concatenate(
            [jnp.where(low, x, jnp.zeros_like(x)), dot(x, shift).astype(BF16)], axis=0
        )
        left = []
        for pair in range(pairs):
            left.append(
                jnp.concatenate(
                    [
                        jnp.broadcast_to(outs[o : o + 1, :], (per, group)).astype(BF16) * own
                        for o in (2 * pair, 2 * pair + 1)
                    ],
                    axis=1,
                )
            )
        made = (dot(jnp.concatenate(left, axis=0), right) * (1.0 / qlen)).astype(BF16)
        for pair in range(pairs):
            grads[g * per : (g + 1) * per, pair * lanes : (pair + 1) * lanes] = made[
                pair * per : (pair + 1) * per, :
            ]

    queries = grads.shape[0]
    precond = dot_nt(high_ref[...], grads[...]) + dot_nt(low_ref[...], grads[...])
    precond = precond.astype(BF16)

    start = pl.multiple_of(me * block, block)
    square = dot(grads[:, pl.ds(start, block)], precond)
    eye = iota((queries, queries), 0) == iota((queries, queries), 1)
    self_inf = jnp.sum(jnp.where(eye, square, 0.0), axis=0, keepdims=True)

    rows = n * tile
    t = train[...].reshape(rows, lanes)
    where = iota((rows, lanes), 0) % tile // number
    wide = jnp.concatenate(
        [jnp.where(where == j, t, 0.0).astype(BF16) for j in range(local)], axis=1
    )
    parts = dot(wide, precond)
    raw = parts
    for j in range(1, local):
        raw = raw + pltpu.roll(parts, rows - j * number, 0)
    raw = jnp.where(iota((rows, queries), 0) % tile < number, raw, self_inf)
    out_ref[...] = jnp.zeros_like(out_ref)
    out_ref[:, :queries] = raw


def score(me, n, number, qlen, slots, pieces, high, low):
    block, coords = high.shape
    lanes = pieces[0].shape[2]
    local = block // lanes
    tokens = pieces[0].shape[1] - INNER * local * number
    queries = n * tokens // qlen
    padded = -(-queries // 128) * 128
    return pl.pallas_call(
        functools.partial(score_kernel, n, number, qlen, slots),
        out_shape=pltpu.VMEM((n * local * number, padded), F32),
        in_specs=[pl.BlockSpec(memory_space=pltpu.SMEM)] + [VMEM] * (len(pieces) + 2),
        out_specs=VMEM,
        scratch_shapes=[
            pltpu.VMEM((n * tokens, lanes), BF16),
            pltpu.VMEM((n, local * number, lanes), F32),
            pltpu.VMEM((queries, coords), BF16),
        ],
        compiler_params=pltpu.CompilerParams(vmem_limit_bytes=20 * 2**20),
        name="score",
    )(me, *pieces, high, low)


def finish_kernel(number, parts_ref, out_ref):
    total = jnp.sum(parts_ref[...], axis=0)
    queries = out_ref.shape[1]
    self_inf = total[number : number + 1, :queries]
    out_ref[...] = total[:number, :queries] / jnp.sqrt(self_inf)


def swap(x, k, n):
    return lax.ppermute(x, "dp", [(i, i ^ k) for i in range(n)])


def fast(n, train_hidden, train_cot, query_hidden, query_cot, proj_in, proj_out, hess_inv):
    number, qlen = train_hidden.shape[0], query_hidden.shape[1]
    queries = n * query_hidden.shape[0]
    planes = n // INNER
    me = lax.axis_index("dp").astype(jnp.int32).reshape(1)
    messages = project(
        me, planes, train_hidden, train_cot, query_hidden, query_cot, proj_in, proj_out
    )
    high, low = split(hess_inv, messages[0])
    got = [messages[0]] + [None] * (planes - 1)
    for k in range(planes - 1, 0, -1):
        got[k] = swap(messages[k], INNER * k, n)
    slots = [INNER * k for k in range(planes)]
    mine, high, low = lax.optimization_barrier((jnp.stack(got), high, low))
    for k in (2, 1):
        mine = jnp.concatenate([mine, swap(mine, k, n)], axis=0)
        slots += [slot ^ k for slot in slots]
    parts = score(me, n, number, qlen, slots, [mine], high, low)
    parts = parts.reshape(n, -1, parts.shape[1])
    parts = lax.all_to_all(parts, "dp", 0, 0, tiled=True)
    return pl.pallas_call(
        functools.partial(finish_kernel, number),
        out_shape=jax.ShapeDtypeStruct((number, queries), F32),
        in_specs=[VMEM],
        out_specs=VMEM,
        compiler_params=pltpu.CompilerParams(vmem_limit_bytes=4 * 2**20),
        name="finish",
    )(pltpu.with_memory_space_constraint(parts, pltpu.VMEM))


def suits(n, args):
    train_hidden, _, query_hidden, _, proj_in, _, hess_inv = args
    number, qlen = train_hidden.shape[0], query_hidden.shape[1]
    tokens = query_hidden.shape[0] * qlen
    lanes = 2 * proj_in.shape[0]
    block = hess_inv.shape[0]
    planes = n // INNER
    return (
        n % INNER == 0
        and planes > 1
        and planes & (planes - 1) == 0
        and lanes == 128
        and block % lanes == 0
        and block // lanes * number == 8
        and tokens % 16 == 0
        and GROUP % (16 * qlen) == 0
        and n * tokens % GROUP == 0
    )


def on_device(n, *args):
    return fast(n, *args) if suits(n, args) else general(*args)


def solution(mesh):
    n = mesh.shape["dp"]
    in_specs = (
        P(("groups", "dp"), None, None),
        P(("groups", "dp"), None, None),
        P(("groups", "dp"), None, None),
        P(("groups", "dp"), None, None),
        P(),
        P(),
        P(("groups", "dp"), None),
    )
    out_specs = P(("groups", "dp"), None)
    return jax.shard_map(
        functools.partial(on_device, n),
        mesh=mesh,
        in_specs=in_specs,
        out_specs=out_specs,
        check_vma=False,
    )
```

```python
import functools

import jax
import jax.numpy as jnp
from jax import lax
from jax.experimental import pallas as pl
from jax.experimental.pallas import tpu as pltpu
from jax.sharding import PartitionSpec as P

F32, BF16 = jnp.float32, jnp.bfloat16
NT = (((1,), (1,)), ((), ()))
VMEM = pl.BlockSpec(memory_space=pltpu.VMEM)
HBM = pl.BlockSpec(memory_space=pltpu.HBM)
CORES = 2
GROUP = 256


def dot(a, b):
    return jnp.dot(a, b, preferred_element_type=F32)


def dot_nt(a, b):
    return lax.dot_general(a, b, NT, preferred_element_type=F32)


def in_hbm(x):
    return pltpu.with_memory_space_constraint(x, pltpu.HBM)


def iota(shape, dim):
    return lax.broadcasted_iota(jnp.int32, shape, dim)


def example_grads(hidden, cotangent, proj_in, proj_out):
    number, length, inner = hidden.shape
    outer_width = cotangent.shape[2]
    rank = proj_in.shape[0]
    inputs = jnp.dot(
        hidden.reshape(number * length, inner), proj_in.T, preferred_element_type=jnp.float32
    ).astype(jnp.bfloat16)
    outputs = jnp.dot(
        cotangent.reshape(number * length, outer_width),
        proj_out.T,
        preferred_element_type=jnp.float32,
    ).astype(jnp.bfloat16)
    inputs = inputs.reshape(number, length, rank)
    outputs = outputs.reshape(number, length, rank)
    summed = jnp.einsum("sto,sti->soi", outputs, inputs, preferred_element_type=jnp.float32) * (
        1.0 / length
    )
    return summed.astype(jnp.bfloat16).reshape(number, rank * rank)


def general(train_hidden, train_cot, query_hidden, query_cot, proj_in, proj_out, hess_inv):
    train_grads = example_grads(train_hidden, train_cot, proj_in, proj_out)
    query_grads = example_grads(query_hidden, query_cot, proj_in, proj_out)
    full_query = lax.all_gather(query_grads, "dp", axis=0, tiled=True).astype(jnp.float32)
    product = jnp.dot(full_query, hess_inv.T, precision=lax.Precision.HIGHEST)
    full_precond = lax.all_gather(product.astype(jnp.bfloat16), "dp", axis=1, tiled=True)
    self_inf = jnp.sum(full_query * full_precond.astype(jnp.float32), axis=1)
    raw = jnp.dot(train_grads, full_precond.T, preferred_element_type=jnp.float32)
    return raw / jnp.sqrt(self_inf)[None, :]


def project_kernel(
    number, length, widths, th_ref, tc_ref, qh_ref, qc_ref, pi_ref, po_ref, out_ref, *scratch
):
    th, tc, qh, qc, pi, po, sems = scratch
    inner = th.shape[1]
    rank = pi.shape[0]
    tokens = th.shape[0]
    queries = qh.shape[0]

    copies = []

    def load(*pairs):
        group = []
        for src, dst in pairs:
            group.append(pltpu.make_async_copy(src, dst, sems.at[sum(map(len, copies)) + len(group)]))
            group[-1].start()
        copies.append(group)

    def arrived():
        for copy in copies.pop(0):
            copy.wait()

    parts = [slice(sum(widths[:c]), sum(widths[: c + 1])) for c in range(len(widths))]
    for c, cols in enumerate(parts):
        load(
            (pi_ref.at[:, cols], pi.at[:, cols]),
            (th_ref.at[:, cols], th.at[:, cols]),
            (qh_ref.at[:, cols], qh.at[:, cols]),
        )
        if c == 0:
            load((po_ref, po), (tc_ref, tc), (qc_ref, qc))

    rows = rank // 2 * number
    t_in = jnp.zeros((tokens, rank), F32)
    q_in = jnp.zeros((queries, rank), F32)
    for c, cols in enumerate(parts):
        arrived()
        t_in += dot_nt(th[:, cols], pi[:, cols])
        q_in += dot_nt(qh[:, cols], pi[:, cols])
        if c == 0:
            arrived()
            q_out = dot_nt(qc[...], po[...])
            t_out = dot_nt(po[...], tc[...]).astype(BF16)

    row, col = iota((rows, tokens), 0), iota((rows, tokens), 1)
    own = row % number == col // length
    lefts = []
    for half in range(2):
        pick = iota((rows, rank), 1) == 2 * (iota((rows, rank), 0) // number) + half
        lefts.append(jnp.where(own, dot(pick.astype(BF16), t_out), 0.0).astype(BF16))

    spread = jnp.concatenate([t_in, t_in], axis=1).astype(BF16)
    lane = iota((tokens, 2 * rank), 1)
    total = jnp.zeros((rows, 2 * rank), F32)
    for half in range(2):
        right = jnp.where(lane // rank == half, spread, jnp.zeros_like(spread))
        total += dot(lefts[half], right)
    grads = (total * (1.0 / length)).astype(BF16)
    message = jnp.concatenate([q_in, q_out], axis=1).astype(BF16)

    share = rows // out_ref.shape[0]
    for chip in range(out_ref.shape[0]):
        out_ref[chip, :queries, :] = message
        out_ref[chip, queries:, :] = grads[chip * share : (chip + 1) * share, :]


def project(chips, train_hidden, train_cot, query_hidden, query_cot, proj_in, proj_out):
    number, length, inner = train_hidden.shape
    width = train_cot.shape[2]
    rank = proj_in.shape[0]
    tokens, queries = number * length, query_hidden.shape[0] * query_hidden.shape[1]
    rows = rank // 2 * number
    widths = [2048, 4096, 4096, 4096]
    return pl.pallas_call(
        functools.partial(project_kernel, number, length, widths),
        out_shape=pltpu.VMEM((chips, queries + rows // chips, 2 * rank), BF16),
        in_specs=[HBM] * 6,
        out_specs=VMEM,
        scratch_shapes=[
            pltpu.VMEM((tokens, inner), BF16),
            pltpu.VMEM((tokens, width), BF16),
            pltpu.VMEM((queries, inner), BF16),
            pltpu.VMEM((queries, width), BF16),
            pltpu.VMEM((rank, inner), BF16),
            pltpu.VMEM((rank, width), BF16),
            pltpu.SemaphoreType.DMA((3 * len(widths) + 3,)),
        ],
        compiler_params=pltpu.CompilerParams(vmem_limit_bytes=20 * 2**20),
        name="project",
    )(
        in_hbm(train_hidden.reshape(tokens, inner)),
        in_hbm(train_cot.reshape(tokens, width)),
        in_hbm(query_hidden.reshape(queries, inner)),
        in_hbm(query_cot.reshape(queries, width)),
        in_hbm(proj_in),
        in_hbm(proj_out),
    )


def build(tok, qlen, grads):
    lanes = tok.shape[1]
    rank = lanes // 2
    pairs = rank // 2
    per = GROUP // qlen
    pick = (iota((rank, lanes), 1) == iota((rank, lanes), 0) + rank).astype(BF16)
    shift = (iota((lanes, lanes), 1) == iota((lanes, lanes), 0) + rank).astype(BF16)
    own = (iota((per, GROUP), 1) // qlen == iota((per, GROUP), 0)).astype(BF16)
    low = iota((GROUP, lanes), 1) < rank
    for g in range(tok.shape[0] // GROUP):
        x = tok[g * GROUP : (g + 1) * GROUP, :]
        outs = dot_nt(pick, x)
        right = jnp.concatenate(
            [jnp.where(low, x, jnp.zeros_like(x)), dot(x, shift).astype(BF16)], axis=0
        )
        left = []
        for pair in range(pairs):
            left.append(
                jnp.concatenate(
                    [
                        jnp.broadcast_to(outs[o : o + 1, :], (per, GROUP)).astype(BF16) * own
                        for o in (2 * pair, 2 * pair + 1)
                    ],
                    axis=1,
                )
            )
        made = (dot(jnp.concatenate(left, axis=0), right) * (1.0 / qlen)).astype(BF16)
        for pair in range(pairs):
            grads[g * per : (g + 1) * per, pair * lanes : (pair + 1) * lanes] = made[
                pair * per : (pair + 1) * per, :
            ]


def prepare_kernel(qlen, chunks, mine_ref, hess_ref, grads_ref, high_ref, low_ref, tok, hess, sems):
    width = hess.shape[1] // chunks
    copies = []
    for c in range(chunks):
        cols = pl.ds(c * width, width)
        copies.append(pltpu.make_async_copy(hess_ref.at[:, cols], hess.at[:, cols], sems.at[c]))
        copies[-1].start()
    tokens = tok.shape[0] // mine_ref.shape[0]
    for chip in range(mine_ref.shape[0]):
        tok[chip * tokens : (chip + 1) * tokens, :] = mine_ref[chip, :tokens, :]
    build(tok, qlen, grads_ref)
    for c in range(chunks):
        copies[c].wait()
        cols = slice(c * width, (c + 1) * width)
        h = hess[:, cols]
        high = h.astype(BF16)
        high_ref[:, cols] = high
        low_ref[:, cols] = (h - high.astype(F32)).astype(BF16)


def prepare(tokens, qlen, mine, hess_inv):
    chips, _, lanes = mine.shape
    coords = hess_inv.shape[1]
    chunks = 4
    return pl.pallas_call(
        functools.partial(prepare_kernel, qlen, chunks),
        out_shape=[
            pltpu.VMEM((chips * tokens // qlen, coords), BF16),
            pltpu.VMEM(hess_inv.shape, BF16),
            pltpu.VMEM(hess_inv.shape, BF16),
        ],
        in_specs=[VMEM, HBM],
        out_specs=[VMEM] * 3,
        scratch_shapes=[
            pltpu.VMEM((chips * tokens, lanes), BF16),
            pltpu.VMEM(hess_inv.shape, F32),
            pltpu.SemaphoreType.DMA((chunks,)),
        ],
        compiler_params=pltpu.CompilerParams(vmem_limit_bytes=20 * 2**20),
        name="prepare",
    )(mine, in_hbm(hess_inv))


def score_kernel(number, qlen, me_ref, mine_ref, theirs_ref, made_ref, high_ref, low_ref, *rest):
    out_ref, tok, train, grads = rest
    me = me_ref[0]
    core = me % CORES
    block = high_ref.shape[0]
    chips, _, lanes = mine_ref.shape
    tokens = tok.shape[0] // chips
    each = tokens // qlen
    local = block // lanes
    tile = local * number

    for chip in range(chips):
        tok[chip * tokens : (chip + 1) * tokens, :] = theirs_ref[chip, :tokens, :]
        for ref, which in ((mine_ref, core), (theirs_ref, 1 - core)):
            both = ref[chip, tokens:, :].astype(F32)
            train[CORES * chip + which] = jnp.where(core == 0, both[:tile], both[tile:])
    half = chips * each
    grads[:half, :] = made_ref[...]
    build(tok, qlen, grads.at[half:, :])

    queries = grads.shape[0]
    precond = dot_nt(high_ref[...], grads[...]) + dot_nt(low_ref[...], grads[...])
    row, col = iota((queries, queries), 0), iota((queries, queries), 1)
    from_core = jnp.where(row < half, core, 1 - core)
    place = (row % half // each * CORES + from_core) * each + row % each
    order = place == col
    precond = dot(precond.astype(BF16), order.astype(BF16)).astype(BF16)

    start = pl.multiple_of(me * block, block)
    square = dot(grads[:, pl.ds(start, block)], precond)
    self_inf = jnp.sum(jnp.where(order, square, 0.0), axis=0, keepdims=True)

    rows = CORES * chips * tile
    t = train[...].reshape(rows, lanes)
    where = iota((rows, lanes), 0) % tile // number
    wide = jnp.concatenate(
        [jnp.where(where == j, t, 0.0).astype(BF16) for j in range(local)], axis=1
    )
    parts = dot(wide, precond)
    raw = parts
    for j in range(1, local):
        raw = raw + pltpu.roll(parts, rows - j * number, 0)
    raw = jnp.where(iota((rows, queries), 0) % tile < number, raw, self_inf)
    out_ref[...] = jnp.zeros_like(out_ref)
    out_ref[:, :queries] = raw


def score(me, number, qlen, tokens, mine, theirs, made, high, low):
    block, coords = high.shape
    chips, _, lanes = mine.shape
    tile = block // lanes * number
    n = CORES * chips
    queries = n * tokens // qlen
    padded = -(-queries // 128) * 128
    return pl.pallas_call(
        functools.partial(score_kernel, number, qlen),
        out_shape=pltpu.VMEM((n * tile, padded), F32),
        in_specs=[pl.BlockSpec(memory_space=pltpu.SMEM)] + [VMEM] * 5,
        out_specs=VMEM,
        scratch_shapes=[
            pltpu.VMEM((chips * tokens, lanes), BF16),
            pltpu.VMEM((n, tile, lanes), F32),
            pltpu.VMEM((queries, coords), BF16),
        ],
        compiler_params=pltpu.CompilerParams(vmem_limit_bytes=20 * 2**20),
        name="score",
    )(me, mine, theirs, made, high, low)


def finish_kernel(number, parts_ref, out_ref):
    total = jnp.sum(parts_ref[...], axis=0)
    queries = out_ref.shape[1]
    self_inf = total[number : number + 1, :queries]
    out_ref[...] = total[:number, :queries] / jnp.sqrt(self_inf)


def fast(n, train_hidden, train_cot, query_hidden, query_cot, proj_in, proj_out, hess_inv):
    number, qlen = train_hidden.shape[0], query_hidden.shape[1]
    tokens = query_hidden.shape[0] * qlen
    queries = n * query_hidden.shape[0]
    chips = n // CORES
    me = lax.axis_index("dp").astype(jnp.int32).reshape(1)
    messages = project(
        chips, train_hidden, train_cot, query_hidden, query_cot, proj_in, proj_out
    )
    same_core = [[CORES * chip + core for chip in range(chips)] for core in range(CORES)]
    mine = lax.all_to_all(messages, "dp", 0, 0, tiled=True, axis_index_groups=same_core)
    theirs = lax.ppermute(mine, "dp", [(i, i ^ 1) for i in range(n)])
    made, high, low = prepare(tokens, qlen, mine, hess_inv)
    parts = score(me, number, qlen, tokens, mine, theirs, made, high, low)
    parts = parts.reshape(n, -1, parts.shape[1])
    parts = lax.all_to_all(parts, "dp", 0, 0, tiled=True)
    return pl.pallas_call(
        functools.partial(finish_kernel, number),
        out_shape=jax.ShapeDtypeStruct((number, queries), F32),
        in_specs=[VMEM],
        out_specs=VMEM,
        compiler_params=pltpu.CompilerParams(vmem_limit_bytes=4 * 2**20),
        name="finish",
    )(pltpu.with_memory_space_constraint(parts, pltpu.VMEM))


def suits(n, args):
    train_hidden, _, query_hidden, _, proj_in, _, hess_inv = args
    number, qlen = train_hidden.shape[0], query_hidden.shape[1]
    tokens = query_hidden.shape[0] * qlen
    lanes = 2 * proj_in.shape[0]
    block = hess_inv.shape[0]
    return (
        n % CORES == 0
        and n > CORES
        and lanes == 128
        and block % lanes == 0
        and block // lanes * number == 8
        and tokens % 16 == 0
        and GROUP % (16 * qlen) == 0
        and n // CORES * tokens % GROUP == 0
    )


def on_device(n, *args):
    return fast(n, *args) if suits(n, args) else general(*args)


def solution(mesh):
    n = mesh.shape["dp"]
    in_specs = (
        P(("groups", "dp"), None, None),
        P(("groups", "dp"), None, None),
        P(("groups", "dp"), None, None),
        P(("groups", "dp"), None, None),
        P(),
        P(),
        P(("groups", "dp"), None),
    )
    out_specs = P(("groups", "dp"), None)
    return jax.shard_map(
        functools.partial(on_device, n),
        mesh=mesh,
        in_specs=in_specs,
        out_specs=out_specs,
        check_vma=False,
    )
```

```python
import functools

import jax
import jax.numpy as jnp
from jax import lax
from jax.experimental import pallas as pl
from jax.experimental.pallas import tpu as pltpu
from jax.sharding import PartitionSpec as P

F32, BF16 = jnp.float32, jnp.bfloat16
NT = (((1,), (1,)), ((), ()))
VMEM = pl.BlockSpec(memory_space=pltpu.VMEM)
HBM = pl.BlockSpec(memory_space=pltpu.HBM)
INNER = 4
GROUP = 256


def dot(a, b):
    return jnp.dot(a, b, preferred_element_type=F32)


def dot_nt(a, b):
    return lax.dot_general(a, b, NT, preferred_element_type=F32)


def in_hbm(x):
    return pltpu.with_memory_space_constraint(x, pltpu.HBM)


def iota(shape, dim):
    return lax.broadcasted_iota(jnp.int32, shape, dim)


def example_grads(hidden, cotangent, proj_in, proj_out):
    number, length, inner = hidden.shape
    outer_width = cotangent.shape[2]
    rank = proj_in.shape[0]
    inputs = jnp.dot(
        hidden.reshape(number * length, inner), proj_in.T, preferred_element_type=jnp.float32
    ).astype(jnp.bfloat16)
    outputs = jnp.dot(
        cotangent.reshape(number * length, outer_width),
        proj_out.T,
        preferred_element_type=jnp.float32,
    ).astype(jnp.bfloat16)
    inputs = inputs.reshape(number, length, rank)
    outputs = outputs.reshape(number, length, rank)
    summed = jnp.einsum("sto,sti->soi", outputs, inputs, preferred_element_type=jnp.float32) * (
        1.0 / length
    )
    return summed.astype(jnp.bfloat16).reshape(number, rank * rank)


def general(train_hidden, train_cot, query_hidden, query_cot, proj_in, proj_out, hess_inv):
    train_grads = example_grads(train_hidden, train_cot, proj_in, proj_out)
    query_grads = example_grads(query_hidden, query_cot, proj_in, proj_out)
    full_query = lax.all_gather(query_grads, "dp", axis=0, tiled=True).astype(jnp.float32)
    product = jnp.dot(full_query, hess_inv.T, precision=lax.Precision.HIGHEST)
    full_precond = lax.all_gather(product.astype(jnp.bfloat16), "dp", axis=1, tiled=True)
    self_inf = jnp.sum(full_query * full_precond.astype(jnp.float32), axis=1)
    raw = jnp.dot(train_grads, full_precond.T, preferred_element_type=jnp.float32)
    return raw / jnp.sqrt(self_inf)[None, :]


def project_kernel(
    planes, number, length, widths, me_ref, th_ref, tc_ref, qh_ref, qc_ref, pi_ref, po_ref, *rest
):
    outs, (th, tc, qh, qc, pi, po, grads, sems) = rest[:planes], rest[planes:]
    inner = th.shape[1]
    rank = pi.shape[0]
    tokens = th.shape[0]
    queries = qh.shape[0]

    copies = []

    def load(*pairs):
        group = []
        for src, dst in pairs:
            group.append(pltpu.make_async_copy(src, dst, sems.at[sum(map(len, copies)) + len(group)]))
            group[-1].start()
        copies.append(group)

    def arrived():
        for copy in copies.pop(0):
            copy.wait()

    parts = [slice(sum(widths[:c]), sum(widths[: c + 1])) for c in range(len(widths))]
    for c, cols in enumerate(parts):
        load(
            (pi_ref.at[:, cols], pi.at[:, cols]),
            (th_ref.at[:, cols], th.at[:, cols]),
            (qh_ref.at[:, cols], qh.at[:, cols]),
        )
        if c == 0:
            load((po_ref, po), (tc_ref, tc), (qc_ref, qc))

    rows = rank // 2 * number
    t_in = jnp.zeros((tokens, rank), F32)
    q_in = jnp.zeros((queries, rank), F32)
    for c, cols in enumerate(parts):
        arrived()
        t_in += dot_nt(th[:, cols], pi[:, cols])
        q_in += dot_nt(qh[:, cols], pi[:, cols])
        if c == 0:
            arrived()
            q_out = dot_nt(qc[...], po[...])
            t_out = dot_nt(po[...], tc[...]).astype(BF16)

    row, col = iota((rows, tokens), 0), iota((rows, tokens), 1)
    own = row % number == col // length
    lefts = []
    for half in range(2):
        pick = iota((rows, rank), 1) == 2 * (iota((rows, rank), 0) // number) + half
        lefts.append(jnp.where(own, dot(pick.astype(BF16), t_out), 0.0).astype(BF16))

    spread = jnp.concatenate([t_in, t_in], axis=1).astype(BF16)
    lane = iota((tokens, 2 * rank), 1)
    total = jnp.zeros((rows, 2 * rank), F32)
    for half in range(2):
        right = jnp.where(lane // rank == half, spread, jnp.zeros_like(spread))
        total += dot(lefts[half], right)
    grads[...] = (total * (1.0 / length)).astype(BF16)
    message = jnp.concatenate([q_in, q_out], axis=1).astype(BF16)

    plane = me_ref[0] // INNER
    share = rows // planes
    for k in range(planes):
        outs[k][:queries, :] = message
        first = pl.multiple_of((plane ^ k) * share, share)
        outs[k][queries:, :] = grads[pl.ds(first, share), :]


def project(me, planes, train_hidden, train_cot, query_hidden, query_cot, proj_in, proj_out):
    number, length, inner = train_hidden.shape
    width = train_cot.shape[2]
    rank = proj_in.shape[0]
    tokens, queries = number * length, query_hidden.shape[0] * query_hidden.shape[1]
    rows = rank // 2 * number
    widths = [2048, 4096, 4096, 4096]
    return pl.pallas_call(
        functools.partial(project_kernel, planes, number, length, widths),
        out_shape=[pltpu.VMEM((queries + rows // planes, 2 * rank), BF16)] * planes,
        in_specs=[pl.BlockSpec(memory_space=pltpu.SMEM)] + [HBM] * 6,
        out_specs=[VMEM] * planes,
        scratch_shapes=[
            pltpu.VMEM((tokens, inner), BF16),
            pltpu.VMEM((tokens, width), BF16),
            pltpu.VMEM((queries, inner), BF16),
            pltpu.VMEM((queries, width), BF16),
            pltpu.VMEM((rank, inner), BF16),
            pltpu.VMEM((rank, width), BF16),
            pltpu.VMEM((rows, 2 * rank), BF16),
            pltpu.SemaphoreType.DMA((3 * len(widths) + 3,)),
        ],
        compiler_params=pltpu.CompilerParams(vmem_limit_bytes=20 * 2**20),
        name="project",
    )(
        me,
        in_hbm(train_hidden.reshape(tokens, inner)),
        in_hbm(train_cot.reshape(tokens, width)),
        in_hbm(query_hidden.reshape(queries, inner)),
        in_hbm(query_cot.reshape(queries, width)),
        in_hbm(proj_in),
        in_hbm(proj_out),
    )


def build(tok, qlen, grads):
    lanes = tok.shape[1]
    rank = lanes // 2
    pairs = rank // 2
    per = GROUP // qlen
    pick = (iota((rank, lanes), 1) == iota((rank, lanes), 0) + rank).astype(BF16)
    shift = (iota((lanes, lanes), 1) == iota((lanes, lanes), 0) + rank).astype(BF16)
    own = (iota((per, GROUP), 1) // qlen == iota((per, GROUP), 0)).astype(BF16)
    every = tok[...]
    outs = dot_nt(pick, every)
    moved = dot(every, shift).astype(BF16)
    still = jnp.where(iota(every.shape, 1) < rank, every, jnp.zeros_like(every))
    for g in range(tok.shape[0] // GROUP):
        cols = slice(g * GROUP, (g + 1) * GROUP)
        left = []
        for pair in range(pairs):
            left.append(
                jnp.concatenate(
                    [
                        jnp.broadcast_to(outs[o : o + 1, cols], (per, GROUP)).astype(BF16) * own
                        for o in (2 * pair, 2 * pair + 1)
                    ],
                    axis=1,
                )
            )
        right = jnp.concatenate([still[cols], moved[cols]], axis=0)
        made = (dot(jnp.concatenate(left, axis=0), right) * (1.0 / qlen)).astype(BF16)
        for pair in range(pairs):
            grads[g * per : (g + 1) * per, pair * lanes : (pair + 1) * lanes] = made[
                pair * per : (pair + 1) * per, :
            ]


def split_kernel(chunks, hess_ref, after_ref, high_ref, low_ref, hess, sems):
    width = hess.shape[1] // chunks
    copies = []
    for c in range(chunks):
        cols = pl.ds(c * width, width)
        copies.append(pltpu.make_async_copy(hess_ref.at[:, cols], hess.at[:, cols], sems.at[c]))
        copies[-1].start()
    for c in range(chunks):
        copies[c].wait()
        cols = slice(c * width, (c + 1) * width)
        h = hess[:, cols]
        high = h.astype(BF16)
        high_ref[:, cols] = high
        low_ref[:, cols] = (h - high.astype(F32)).astype(BF16)


def split(hess_inv, after):
    chunks = 4
    return pl.pallas_call(
        functools.partial(split_kernel, chunks),
        out_shape=[pltpu.VMEM(hess_inv.shape, BF16)] * 2,
        in_specs=[HBM, VMEM],
        out_specs=[VMEM] * 2,
        scratch_shapes=[
            pltpu.VMEM(hess_inv.shape, F32),
            pltpu.SemaphoreType.DMA((chunks,)),
        ],
        compiler_params=pltpu.CompilerParams(vmem_limit_bytes=20 * 2**20),
        name="split",
    )(in_hbm(hess_inv), after)


def prepare_kernel(qlen, mine_ref, grads_ref, tok):
    tokens = tok.shape[0] // mine_ref.shape[0]
    for slot in range(mine_ref.shape[0]):
        tok[slot * tokens : (slot + 1) * tokens, :] = mine_ref[slot, :tokens, :]
    build(tok, qlen, grads_ref)


def prepare(tokens, qlen, coords, mine):
    count, _, lanes = mine.shape
    return pl.pallas_call(
        functools.partial(prepare_kernel, qlen),
        out_shape=pltpu.VMEM((count * tokens // qlen, coords), BF16),
        in_specs=[VMEM],
        out_specs=VMEM,
        scratch_shapes=[pltpu.VMEM((count * tokens, lanes), BF16)],
        compiler_params=pltpu.CompilerParams(vmem_limit_bytes=20 * 2**20),
        name="prepare",
    )(mine)


def score_kernel(number, tokens, qlen, me_ref, mine_ref, theirs_ref, *rest):
    made_refs, (high_ref, low_ref, out_ref, train) = rest[:2], rest[2:]
    me = me_ref[0]
    block = high_ref.shape[0]
    count, _, lanes = mine_ref.shape
    planes = count // (INNER // 2)
    each = tokens // qlen
    local = block // lanes
    tile = local * number
    inner = me % INNER

    def source(slot):
        by_two, plane = slot // planes % 2, (planes - slot % planes) % planes
        return me ^ (plane * INNER + by_two * 2 + slot // count)

    for slot in range(count):
        for ref, first in ((mine_ref, 0), (theirs_ref, count)):
            share = ref[slot, tokens:, :].astype(F32)
            picked = share[:tile]
            for j in range(1, INNER):
                picked = jnp.where(inner == j, share[j * tile : (j + 1) * tile], picked)
            train[source(first + slot)] = picked
    grads = jnp.concatenate([ref[...] for ref in made_refs], axis=0)
    queries = grads.shape[0]
    precond = dot_nt(high_ref[...], grads) + dot_nt(low_ref[...], grads)
    row, col = iota((queries, queries), 0), iota((queries, queries), 1)
    order = source(row // each) * each + row % each == col
    precond = dot(precond.astype(BF16), order.astype(BF16)).astype(BF16)

    cols = pl.ds(pl.multiple_of(me * block, block), block)
    square = dot(jnp.concatenate([ref[:, cols] for ref in made_refs], axis=0), precond)
    self_inf = jnp.sum(jnp.where(order, square, 0.0), axis=0, keepdims=True)

    rows = 2 * count * tile
    t = train[...].reshape(rows, lanes)
    where = iota((rows, lanes), 0) % tile // number
    wide = jnp.concatenate(
        [jnp.where(where == j, t, 0.0).astype(BF16) for j in range(local)], axis=1
    )
    parts = dot(wide, precond)
    raw = parts
    for j in range(1, local):
        raw = raw + pltpu.roll(parts, rows - j * number, 0)
    raw = jnp.where(iota((rows, queries), 0) % tile < number, raw, self_inf)
    out_ref[...] = jnp.zeros_like(out_ref)
    out_ref[:, :queries] = raw


def score(me, number, tokens, qlen, mine, theirs, made, high, low):
    block = high.shape[0]
    count, _, lanes = mine.shape
    tile = block // lanes * number
    n = 2 * count
    queries = n * tokens // qlen
    padded = -(-queries // 128) * 128
    return pl.pallas_call(
        functools.partial(score_kernel, number, tokens, qlen),
        out_shape=pltpu.VMEM((n * tile, padded), F32),
        in_specs=[pl.BlockSpec(memory_space=pltpu.SMEM)] + [VMEM] * 6,
        out_specs=VMEM,
        scratch_shapes=[pltpu.VMEM((n, tile, lanes), F32)],
        compiler_params=pltpu.CompilerParams(vmem_limit_bytes=20 * 2**20),
        name="score",
    )(me, mine, theirs, *made, high, low)


def finish_kernel(number, parts_ref, out_ref):
    total = jnp.sum(parts_ref[...], axis=0)
    queries = out_ref.shape[1]
    self_inf = total[number : number + 1, :queries]
    out_ref[...] = total[:number, :queries] / jnp.sqrt(self_inf)


def swap(x, k, n):
    return lax.ppermute(x, "dp", [(i, i ^ k) for i in range(n)])


def fast(n, train_hidden, train_cot, query_hidden, query_cot, proj_in, proj_out, hess_inv):
    number, qlen = train_hidden.shape[0], query_hidden.shape[1]
    tokens = query_hidden.shape[0] * qlen
    queries = n * query_hidden.shape[0]
    planes = n // INNER
    me = lax.axis_index("dp").astype(jnp.int32).reshape(1)
    messages = project(
        me, planes, train_hidden, train_cot, query_hidden, query_cot, proj_in, proj_out
    )
    high, low = split(hess_inv, messages[0])
    got = [messages[0]] + [swap(messages[k], INNER * k, n) for k in range(planes - 1, 0, -1)]
    got, high, low = lax.optimization_barrier((jnp.stack(got), high, low))
    mine = jnp.concatenate([got, swap(got, 2, n)], axis=0)
    theirs = swap(mine, 1, n)
    made = [prepare(tokens, qlen, hess_inv.shape[1], part) for part in (mine, theirs)]
    parts = score(me, number, tokens, qlen, mine, theirs, made, high, low)
    parts = parts.reshape(n, -1, parts.shape[1])
    parts = lax.all_to_all(parts, "dp", 0, 0, tiled=True)
    return pl.pallas_call(
        functools.partial(finish_kernel, number),
        out_shape=jax.ShapeDtypeStruct((number, queries), F32),
        in_specs=[VMEM],
        out_specs=VMEM,
        compiler_params=pltpu.CompilerParams(vmem_limit_bytes=4 * 2**20),
        name="finish",
    )(pltpu.with_memory_space_constraint(parts, pltpu.VMEM))


def suits(n, args):
    train_hidden, _, query_hidden, _, proj_in, _, hess_inv = args
    number, qlen = train_hidden.shape[0], query_hidden.shape[1]
    tokens = query_hidden.shape[0] * qlen
    lanes = 2 * proj_in.shape[0]
    block = hess_inv.shape[0]
    planes = n // INNER
    return (
        n % INNER == 0
        and planes > 1
        and planes & (planes - 1) == 0
        and lanes == 128
        and block % lanes == 0
        and block // lanes * number == 8
        and tokens % 16 == 0
        and GROUP % (16 * qlen) == 0
        and n // 2 * tokens % GROUP == 0
    )


def on_device(n, *args):
    return fast(n, *args) if suits(n, args) else general(*args)


def solution(mesh):
    n = mesh.shape["dp"]
    in_specs = (
        P(("groups", "dp"), None, None),
        P(("groups", "dp"), None, None),
        P(("groups", "dp"), None, None),
        P(("groups", "dp"), None, None),
        P(),
        P(),
        P(("groups", "dp"), None),
    )
    out_specs = P(("groups", "dp"), None)
    return jax.shard_map(
        functools.partial(on_device, n),
        mesh=mesh,
        in_specs=in_specs,
        out_specs=out_specs,
        check_vma=False,
    )
```

```python
import functools

import jax
import jax.numpy as jnp
from jax import lax
from jax.experimental import pallas as pl
from jax.experimental.pallas import tpu as pltpu
from jax.sharding import PartitionSpec as P

F32, BF16 = jnp.float32, jnp.bfloat16
NT = (((1,), (1,)), ((), ()))
VMEM = pl.BlockSpec(memory_space=pltpu.VMEM)
HBM = pl.BlockSpec(memory_space=pltpu.HBM)
INNER = 4
GROUP = 128


def dot(a, b):
    return jnp.dot(a, b, preferred_element_type=F32)


def dot_nt(a, b):
    return lax.dot_general(a, b, NT, preferred_element_type=F32)


def in_hbm(x):
    return pltpu.with_memory_space_constraint(x, pltpu.HBM)


def iota(shape, dim):
    return lax.broadcasted_iota(jnp.int32, shape, dim)


def example_grads(hidden, cotangent, proj_in, proj_out):
    number, length, inner = hidden.shape
    outer_width = cotangent.shape[2]
    rank = proj_in.shape[0]
    inputs = jnp.dot(
        hidden.reshape(number * length, inner), proj_in.T, preferred_element_type=jnp.float32
    ).astype(jnp.bfloat16)
    outputs = jnp.dot(
        cotangent.reshape(number * length, outer_width),
        proj_out.T,
        preferred_element_type=jnp.float32,
    ).astype(jnp.bfloat16)
    inputs = inputs.reshape(number, length, rank)
    outputs = outputs.reshape(number, length, rank)
    summed = jnp.einsum("sto,sti->soi", outputs, inputs, preferred_element_type=jnp.float32) * (
        1.0 / length
    )
    return summed.astype(jnp.bfloat16).reshape(number, rank * rank)


def general(train_hidden, train_cot, query_hidden, query_cot, proj_in, proj_out, hess_inv):
    train_grads = example_grads(train_hidden, train_cot, proj_in, proj_out)
    query_grads = example_grads(query_hidden, query_cot, proj_in, proj_out)
    full_query = lax.all_gather(query_grads, "dp", axis=0, tiled=True).astype(jnp.float32)
    product = jnp.dot(full_query, hess_inv.T, precision=lax.Precision.HIGHEST)
    full_precond = lax.all_gather(product.astype(jnp.bfloat16), "dp", axis=1, tiled=True)
    self_inf = jnp.sum(full_query * full_precond.astype(jnp.float32), axis=1)
    raw = jnp.dot(train_grads, full_precond.T, preferred_element_type=jnp.float32)
    return raw / jnp.sqrt(self_inf)[None, :]


def project_kernel(
    planes, number, length, widths, me_ref, th_ref, tc_ref, qh_ref, qc_ref, pi_ref, po_ref, *rest
):
    outs, (th, tc, qh, qc, pi, po, grads, sems) = rest[:planes], rest[planes:]
    inner = th.shape[1]
    rank = pi.shape[0]
    tokens = th.shape[0]
    queries = qh.shape[0]

    copies = []

    def load(*pairs):
        group = []
        for src, dst in pairs:
            group.append(pltpu.make_async_copy(src, dst, sems.at[sum(map(len, copies)) + len(group)]))
            group[-1].start()
        copies.append(group)

    def arrived():
        for copy in copies.pop(0):
            copy.wait()

    parts = [slice(sum(widths[:c]), sum(widths[: c + 1])) for c in range(len(widths))]
    for c, cols in enumerate(parts):
        load(
            (pi_ref.at[:, cols], pi.at[:, cols]),
            (th_ref.at[:, cols], th.at[:, cols]),
            (qh_ref.at[:, cols], qh.at[:, cols]),
        )
        if c == 0:
            load((po_ref, po), (tc_ref, tc), (qc_ref, qc))

    rows = rank // 2 * number
    t_in = jnp.zeros((tokens, rank), F32)
    q_in = jnp.zeros((queries, rank), F32)
    for c, cols in enumerate(parts):
        arrived()
        t_in += dot_nt(th[:, cols], pi[:, cols])
        q_in += dot_nt(qh[:, cols], pi[:, cols])
        if c == 0:
            arrived()
            q_out = dot_nt(qc[...], po[...])
            t_out = dot_nt(po[...], tc[...]).astype(BF16)

    row, col = iota((rows, tokens), 0), iota((rows, tokens), 1)
    own = row % number == col // length
    lefts = []
    for half in range(2):
        pick = iota((rows, rank), 1) == 2 * (iota((rows, rank), 0) // number) + half
        lefts.append(jnp.where(own, dot(pick.astype(BF16), t_out), 0.0).astype(BF16))

    spread = jnp.concatenate([t_in, t_in], axis=1).astype(BF16)
    lane = iota((tokens, 2 * rank), 1)
    total = jnp.zeros((rows, 2 * rank), F32)
    for half in range(2):
        right = jnp.where(lane // rank == half, spread, jnp.zeros_like(spread))
        total += dot(lefts[half], right)
    grads[...] = (total * (1.0 / length)).astype(BF16)
    message = jnp.concatenate([q_in, q_out], axis=1).astype(BF16)

    plane = me_ref[0] // INNER
    share = rows // planes
    for k in range(planes):
        outs[k][:queries, :] = message
        first = pl.multiple_of((plane ^ k) * share, share)
        outs[k][queries:, :] = grads[pl.ds(first, share), :]


def project(me, planes, train_hidden, train_cot, query_hidden, query_cot, proj_in, proj_out):
    number, length, inner = train_hidden.shape
    width = train_cot.shape[2]
    rank = proj_in.shape[0]
    tokens, queries = number * length, query_hidden.shape[0] * query_hidden.shape[1]
    rows = rank // 2 * number
    widths = [2048, 4096, 4096, 4096]
    return pl.pallas_call(
        functools.partial(project_kernel, planes, number, length, widths),
        out_shape=[pltpu.VMEM((queries + rows // planes, 2 * rank), BF16)] * planes,
        in_specs=[pl.BlockSpec(memory_space=pltpu.SMEM)] + [HBM] * 6,
        out_specs=[VMEM] * planes,
        scratch_shapes=[
            pltpu.VMEM((tokens, inner), BF16),
            pltpu.VMEM((tokens, width), BF16),
            pltpu.VMEM((queries, inner), BF16),
            pltpu.VMEM((queries, width), BF16),
            pltpu.VMEM((rank, inner), BF16),
            pltpu.VMEM((rank, width), BF16),
            pltpu.VMEM((rows, 2 * rank), BF16),
            pltpu.SemaphoreType.DMA((3 * len(widths) + 3,)),
        ],
        compiler_params=pltpu.CompilerParams(vmem_limit_bytes=20 * 2**20),
        name="project",
    )(
        me,
        in_hbm(train_hidden.reshape(tokens, inner)),
        in_hbm(train_cot.reshape(tokens, width)),
        in_hbm(query_hidden.reshape(queries, inner)),
        in_hbm(query_cot.reshape(queries, width)),
        in_hbm(proj_in),
        in_hbm(proj_out),
    )


def build(tok, qlen, grads):
    lanes = tok.shape[1]
    rank = lanes // 2
    pairs = rank // 2
    per = GROUP // qlen
    groups = tok.shape[0] // GROUP
    pick = (iota((rank, lanes), 1) == iota((rank, lanes), 0) + rank).astype(BF16)
    shift = (iota((lanes, lanes), 1) == iota((lanes, lanes), 0) + rank).astype(BF16)
    own = iota((per, GROUP), 1) // qlen == iota((per, GROUP), 0)
    every = tok[...]
    outs = dot_nt(pick, every)
    moved = dot(every, shift).astype(BF16)
    still = jnp.where(iota(every.shape, 1) < rank, every, jnp.zeros_like(every))
    made = []
    for g in range(groups):
        cols = slice(g * GROUP, (g + 1) * GROUP)
        left = [
            jnp.concatenate(
                [
                    jnp.where(own, jnp.broadcast_to(outs[o : o + 1, cols], own.shape), 0.0)
                    for o in range(half, rank, 2)
                ],
                axis=0,
            ).astype(BF16)
            for half in range(2)
        ]
        right = jnp.concatenate([still[cols], moved[cols]], axis=0)
        made.append(dot(jnp.concatenate(left, axis=1), right) * (1.0 / qlen))
    made += [jnp.zeros_like(made[0])] * (groups % 2)
    for g in range(0, groups, 2):
        for pair in range(pairs):
            rows = slice(pair * per, (pair + 1) * per)
            grads[g * per : (g + 2) * per, pair * lanes : (pair + 1) * lanes] = jnp.concatenate(
                [made[g][rows], made[g + 1][rows]], axis=0
            ).astype(BF16)


def split_kernel(chunks, hess_ref, after_ref, high_ref, low_ref, hess, sems):
    width = hess.shape[1] // chunks
    copies = []
    for c in range(chunks):
        cols = pl.ds(c * width, width)
        copies.append(pltpu.make_async_copy(hess_ref.at[:, cols], hess.at[:, cols], sems.at[c]))
        copies[-1].start()
    for c in range(chunks):
        copies[c].wait()
        cols = slice(c * width, (c + 1) * width)
        h = hess[:, cols]
        high = h.astype(BF16)
        high_ref[:, cols] = high
        low_ref[:, cols] = (h - high.astype(F32)).astype(BF16)


def split(hess_inv, after):
    chunks = 4
    return pl.pallas_call(
        functools.partial(split_kernel, chunks),
        out_shape=[pltpu.VMEM(hess_inv.shape, BF16)] * 2,
        in_specs=[HBM, VMEM],
        out_specs=[VMEM] * 2,
        scratch_shapes=[
            pltpu.VMEM(hess_inv.shape, F32),
            pltpu.SemaphoreType.DMA((chunks,)),
        ],
        compiler_params=pltpu.CompilerParams(vmem_limit_bytes=20 * 2**20),
        name="split",
    )(in_hbm(hess_inv), after)


def prepare_kernel(tokens, qlen, *refs):
    pieces, (grads_ref, tok) = refs[:-2], refs[-2:]
    first = 0
    for piece in pieces:
        for part in range(piece.shape[0]):
            tok[first : first + tokens, :] = piece[part, :tokens, :]
            first += tokens
    build(tok, qlen, grads_ref)


def prepare(tokens, qlen, coords, *pieces):
    total = sum(piece.shape[0] for piece in pieces) * tokens
    rows = -(-total // (2 * GROUP)) * (2 * GROUP) // qlen
    return pl.pallas_call(
        functools.partial(prepare_kernel, tokens, qlen),
        out_shape=pltpu.VMEM((rows, coords), BF16),
        in_specs=[VMEM] * len(pieces),
        out_specs=VMEM,
        scratch_shapes=[pltpu.VMEM((total, pieces[0].shape[2]), BF16)],
        compiler_params=pltpu.CompilerParams(vmem_limit_bytes=20 * 2**20),
        name="prepare",
    )(*pieces)


def score_kernel(number, tokens, qlen, slots, rows_of, me_ref, *refs):
    pieces, refs = refs[: len(slots)], refs[len(slots) :]
    made_refs, (high_ref, low_ref, out_ref, train) = refs[: len(rows_of)], refs[len(rows_of) :]
    me = me_ref[0]
    block = high_ref.shape[0]
    n, tile, lanes = train.shape
    each = tokens // qlen
    queries = n * each
    local = block // lanes
    inner = me % INNER

    for piece, froms in zip(pieces, slots):
        for part, slot in enumerate(froms):
            share = piece[part, tokens:, :].astype(F32)
            picked = share[:tile]
            for j in range(1, INNER):
                picked = jnp.where(inner == j, share[j * tile : (j + 1) * tile], picked)
            train[me ^ slot] = picked
    grads = jnp.concatenate([ref[...] for ref in made_refs], axis=0)
    precond = dot_nt(high_ref[...], grads) + dot_nt(low_ref[...], grads)
    row, col = iota((grads.shape[0], queries), 0), iota((grads.shape[0], queries), 1)
    place = jnp.full(row.shape, -1, jnp.int32)
    first = 0
    for ref, froms in zip(made_refs, rows_of):
        for i, slot in enumerate(froms):
            at = row - (first + i * each)
            place = jnp.where((at >= 0) & (at < each), (me ^ slot) * each + at, place)
        first += ref.shape[0]
    order = place == col
    precond = dot(precond.astype(BF16), order.astype(BF16)).astype(BF16)

    cols = pl.ds(pl.multiple_of(me * block, block), block)
    square = dot(jnp.concatenate([ref[:, cols] for ref in made_refs], axis=0), precond)
    self_inf = jnp.sum(jnp.where(order, square, 0.0), axis=0, keepdims=True)

    rows = n * tile
    t = train[...].reshape(rows, lanes)
    where = iota((rows, lanes), 0) % tile // number
    wide = jnp.concatenate(
        [jnp.where(where == j, t, 0.0).astype(BF16) for j in range(local)], axis=1
    )
    parts = dot(wide, precond)
    raw = parts
    for j in range(1, local):
        raw = raw + pltpu.roll(parts, rows - j * number, 0)
    raw = jnp.where(iota((rows, queries), 0) % tile < number, raw, self_inf)
    out_ref[...] = jnp.zeros_like(out_ref)
    out_ref[:, :queries] = raw


def score(me, number, tokens, qlen, pieces, slots, made, rows_of, high, low):
    block = high.shape[0]
    lanes = pieces[0].shape[2]
    tile = block // lanes * number
    n = sum(map(len, slots))
    queries = n * tokens // qlen
    padded = -(-queries // 128) * 128
    return pl.pallas_call(
        functools.partial(score_kernel, number, tokens, qlen, slots, rows_of),
        out_shape=pltpu.VMEM((n * tile, padded), F32),
        in_specs=[pl.BlockSpec(memory_space=pltpu.SMEM)] + [VMEM] * (len(pieces) + len(made) + 2),
        out_specs=VMEM,
        scratch_shapes=[pltpu.VMEM((n, tile, lanes), F32)],
        compiler_params=pltpu.CompilerParams(vmem_limit_bytes=20 * 2**20),
        name="score",
    )(me, *pieces, *made, high, low)


def finish_kernel(number, parts_ref, out_ref):
    total = jnp.sum(parts_ref[...], axis=0)
    queries = out_ref.shape[1]
    self_inf = total[number : number + 1, :queries]
    out_ref[...] = total[:number, :queries] / jnp.sqrt(self_inf)


def swap(x, k, n):
    return lax.ppermute(x, "dp", [(i, i ^ k) for i in range(n)])


def fast(n, train_hidden, train_cot, query_hidden, query_cot, proj_in, proj_out, hess_inv):
    number, qlen = train_hidden.shape[0], query_hidden.shape[1]
    tokens = query_hidden.shape[0] * qlen
    queries = n * query_hidden.shape[0]
    planes = n // INNER
    me = lax.axis_index("dp").astype(jnp.int32).reshape(1)
    messages = project(
        me, planes, train_hidden, train_cot, query_hidden, query_cot, proj_in, proj_out
    )
    coords = hess_inv.shape[1]
    others = [INNER * k for k in range(planes - 1, 0, -1)]
    far = [swap(messages[slot // INNER], slot, n) for slot in others]
    own_two = swap(messages[0], 2, n)
    by_plane = jnp.stack([messages[0]] + far)
    by_plane_one = swap(by_plane, 1, n)
    by_two = jnp.concatenate([own_two[None], swap(by_plane[1:], 2, n)], axis=0)
    high, low = split(hess_inv, by_plane)
    made = [prepare(tokens, qlen, coords, by_plane, by_plane_one)]
    by_two, high, low = lax.optimization_barrier((by_two, high, low))
    by_two_one = swap(by_two, 1, n)
    made += [prepare(tokens, qlen, coords, by_two), prepare(tokens, qlen, coords, by_two_one)]
    slots = [[first ^ slot for slot in [0] + others] for first in (0, 1, 2, 3)]
    rows_of = [slots[0] + slots[1], slots[2], slots[3]]
    pieces = [by_plane, by_plane_one, by_two, by_two_one]
    parts = score(me, number, tokens, qlen, pieces, slots, made, rows_of, high, low)
    parts = parts.reshape(n, -1, parts.shape[1])
    parts = lax.all_to_all(parts, "dp", 0, 0, tiled=True)
    return pl.pallas_call(
        functools.partial(finish_kernel, number),
        out_shape=jax.ShapeDtypeStruct((number, queries), F32),
        in_specs=[VMEM],
        out_specs=VMEM,
        compiler_params=pltpu.CompilerParams(vmem_limit_bytes=4 * 2**20),
        name="finish",
    )(pltpu.with_memory_space_constraint(parts, pltpu.VMEM))


def suits(n, args):
    train_hidden, _, query_hidden, _, proj_in, _, hess_inv = args
    number, qlen = train_hidden.shape[0], query_hidden.shape[1]
    tokens = query_hidden.shape[0] * qlen
    lanes = 2 * proj_in.shape[0]
    block = hess_inv.shape[0]
    planes = n // INNER
    return (
        n % INNER == 0
        and planes > 1
        and planes & (planes - 1) == 0
        and lanes == 128
        and block % lanes == 0
        and block // lanes * number == 8
        and tokens % 16 == 0
        and GROUP == 8 * qlen
        and planes * tokens % GROUP == 0
        and 2 * planes * tokens % (2 * GROUP) == 0
    )


def on_device(n, *args):
    return fast(n, *args) if suits(n, args) else general(*args)


def solution(mesh):
    n = mesh.shape["dp"]
    in_specs = (
        P(("groups", "dp"), None, None),
        P(("groups", "dp"), None, None),
        P(("groups", "dp"), None, None),
        P(("groups", "dp"), None, None),
        P(),
        P(),
        P(("groups", "dp"), None),
    )
    out_specs = P(("groups", "dp"), None)
    return jax.shard_map(
        functools.partial(on_device, n),
        mesh=mesh,
        in_specs=in_specs,
        out_specs=out_specs,
        check_vma=False,
    )
```

```python
import functools

import jax
import jax.numpy as jnp
from jax import lax
from jax.experimental import pallas as pl
from jax.experimental.pallas import tpu as pltpu
from jax.sharding import PartitionSpec as P

F32, BF16 = jnp.float32, jnp.bfloat16
NT = (((1,), (1,)), ((), ()))
VMEM = pl.BlockSpec(memory_space=pltpu.VMEM)
HBM = pl.BlockSpec(memory_space=pltpu.HBM)
INNER = 4
GROUP = 128


def dot(a, b):
    return jnp.dot(a, b, preferred_element_type=F32)


def dot_nt(a, b):
    return lax.dot_general(a, b, NT, preferred_element_type=F32)


def in_hbm(x):
    return pltpu.with_memory_space_constraint(x, pltpu.HBM)


def iota(shape, dim):
    return lax.broadcasted_iota(jnp.int32, shape, dim)


def example_grads(hidden, cotangent, proj_in, proj_out):
    number, length, inner = hidden.shape
    outer_width = cotangent.shape[2]
    rank = proj_in.shape[0]
    inputs = jnp.dot(
        hidden.reshape(number * length, inner), proj_in.T, preferred_element_type=jnp.float32
    ).astype(jnp.bfloat16)
    outputs = jnp.dot(
        cotangent.reshape(number * length, outer_width),
        proj_out.T,
        preferred_element_type=jnp.float32,
    ).astype(jnp.bfloat16)
    inputs = inputs.reshape(number, length, rank)
    outputs = outputs.reshape(number, length, rank)
    summed = jnp.einsum("sto,sti->soi", outputs, inputs, preferred_element_type=jnp.float32) * (
        1.0 / length
    )
    return summed.astype(jnp.bfloat16).reshape(number, rank * rank)


def general(train_hidden, train_cot, query_hidden, query_cot, proj_in, proj_out, hess_inv):
    train_grads = example_grads(train_hidden, train_cot, proj_in, proj_out)
    query_grads = example_grads(query_hidden, query_cot, proj_in, proj_out)
    full_query = lax.all_gather(query_grads, "dp", axis=0, tiled=True).astype(jnp.float32)
    product = jnp.dot(full_query, hess_inv.T, precision=lax.Precision.HIGHEST)
    full_precond = lax.all_gather(product.astype(jnp.bfloat16), "dp", axis=1, tiled=True)
    self_inf = jnp.sum(full_query * full_precond.astype(jnp.float32), axis=1)
    raw = jnp.dot(train_grads, full_precond.T, preferred_element_type=jnp.float32)
    return raw / jnp.sqrt(self_inf)[None, :]


def project_kernel(
    planes, number, length, widths, me_ref, th_ref, tc_ref, qh_ref, qc_ref, pi_ref, po_ref, *rest
):
    outs, (th, tc, qh, qc, pi, po, grads, sems) = rest[:planes], rest[planes:]
    inner = th.shape[1]
    rank = pi.shape[0]
    tokens = th.shape[0]
    queries = qh.shape[0]

    copies = []

    def load(*pairs):
        group = []
        for src, dst in pairs:
            group.append(pltpu.make_async_copy(src, dst, sems.at[sum(map(len, copies)) + len(group)]))
            group[-1].start()
        copies.append(group)

    def arrived():
        for copy in copies.pop(0):
            copy.wait()

    parts = [slice(sum(widths[:c]), sum(widths[: c + 1])) for c in range(len(widths))]
    for c, cols in enumerate(parts):
        load(
            (pi_ref.at[:, cols], pi.at[:, cols]),
            (th_ref.at[:, cols], th.at[:, cols]),
            (qh_ref.at[:, cols], qh.at[:, cols]),
        )
        if c == 0:
            load((po_ref, po), (tc_ref, tc), (qc_ref, qc))

    rows = rank // 2 * number
    t_in = jnp.zeros((tokens, rank), F32)
    q_in = jnp.zeros((queries, rank), F32)
    for c, cols in enumerate(parts):
        arrived()
        t_in += dot_nt(th[:, cols], pi[:, cols])
        q_in += dot_nt(qh[:, cols], pi[:, cols])
        if c == 0:
            arrived()
            q_out = dot_nt(qc[...], po[...])
            t_out = dot_nt(po[...], tc[...]).astype(BF16)

    row, col = iota((rows, tokens), 0), iota((rows, tokens), 1)
    own = row % number == col // length
    lefts = []
    for half in range(2):
        pick = iota((rows, rank), 1) == 2 * (iota((rows, rank), 0) // number) + half
        lefts.append(jnp.where(own, dot(pick.astype(BF16), t_out), 0.0).astype(BF16))

    spread = jnp.concatenate([t_in, t_in], axis=1).astype(BF16)
    lane = iota((tokens, 2 * rank), 1)
    total = jnp.zeros((rows, 2 * rank), F32)
    for half in range(2):
        right = jnp.where(lane // rank == half, spread, jnp.zeros_like(spread))
        total += dot(lefts[half], right)
    grads[...] = total * (1.0 / length)
    message = jnp.concatenate([q_in, q_out], axis=1).astype(BF16)

    plane, inner = me_ref[0] // INNER, me_ref[0] % INNER
    tile = rows // planes // INNER
    edge = 2 * tile
    for k in range(planes):
        shares = [
            grads[pl.ds(pl.multiple_of(((plane ^ k) * INNER + (inner ^ j)) * tile, tile), tile), :]
            for j in (0, 1, 3, 2)
        ]
        outs[k][:edge, :] = jnp.concatenate(shares[:2], axis=0).astype(BF16)
        outs[k][edge : edge + queries, :] = message
        outs[k][edge + queries :, :] = jnp.concatenate(shares[2:], axis=0).astype(BF16)


def project(me, planes, train_hidden, train_cot, query_hidden, query_cot, proj_in, proj_out):
    number, length, inner = train_hidden.shape
    width = train_cot.shape[2]
    rank = proj_in.shape[0]
    tokens, queries = number * length, query_hidden.shape[0] * query_hidden.shape[1]
    rows = rank // 2 * number
    widths = [2048, 4096, 4096, 4096]
    return pl.pallas_call(
        functools.partial(project_kernel, planes, number, length, widths),
        out_shape=[pltpu.VMEM((queries + rows // planes, 2 * rank), BF16)] * planes,
        in_specs=[pl.BlockSpec(memory_space=pltpu.SMEM)] + [HBM] * 6,
        out_specs=[VMEM] * planes,
        scratch_shapes=[
            pltpu.VMEM((tokens, inner), BF16),
            pltpu.VMEM((tokens, width), BF16),
            pltpu.VMEM((queries, inner), BF16),
            pltpu.VMEM((queries, width), BF16),
            pltpu.VMEM((rank, inner), BF16),
            pltpu.VMEM((rank, width), BF16),
            pltpu.VMEM((rows, 2 * rank), F32),
            pltpu.SemaphoreType.DMA((3 * len(widths) + 3,)),
        ],
        compiler_params=pltpu.CompilerParams(vmem_limit_bytes=20 * 2**20),
        name="project",
    )(
        me,
        in_hbm(train_hidden.reshape(tokens, inner)),
        in_hbm(train_cot.reshape(tokens, width)),
        in_hbm(query_hidden.reshape(queries, inner)),
        in_hbm(query_cot.reshape(queries, width)),
        in_hbm(proj_in),
        in_hbm(proj_out),
    )


def build(tok, qlen, grads):
    lanes = tok.shape[1]
    rank = lanes // 2
    pairs = rank // 2
    per = GROUP // qlen
    groups = tok.shape[0] // GROUP
    pick = (iota((rank, lanes), 1) == iota((rank, lanes), 0) + rank).astype(BF16)
    shift = (iota((lanes, lanes), 1) == iota((lanes, lanes), 0) + rank).astype(BF16)
    own = iota((per, GROUP), 1) // qlen == iota((per, GROUP), 0)
    every = tok[...]
    outs = dot_nt(pick, every)
    moved = dot(every, shift).astype(BF16)
    still = jnp.where(iota(every.shape, 1) < rank, every, jnp.zeros_like(every))
    made = []
    for g in range(groups):
        cols = slice(g * GROUP, (g + 1) * GROUP)
        left = [
            jnp.concatenate(
                [
                    jnp.where(own, jnp.broadcast_to(outs[o : o + 1, cols], own.shape), 0.0)
                    for o in range(half, rank, 2)
                ],
                axis=0,
            ).astype(BF16)
            for half in range(2)
        ]
        right = jnp.concatenate([still[cols], moved[cols]], axis=0)
        made.append(dot(jnp.concatenate(left, axis=1), right) * (1.0 / qlen))
    made += [jnp.zeros_like(made[0])] * (groups % 2)
    for g in range(0, groups, 2):
        for pair in range(pairs):
            rows = slice(pair * per, (pair + 1) * per)
            grads[g * per : (g + 2) * per, pair * lanes : (pair + 1) * lanes] = jnp.concatenate(
                [made[g][rows], made[g + 1][rows]], axis=0
            ).astype(BF16)


def split_kernel(chunks, hess_ref, after_ref, high_ref, low_ref, hess, sems):
    width = hess.shape[1] // chunks
    copies = []
    for c in range(chunks):
        cols = pl.ds(c * width, width)
        copies.append(pltpu.make_async_copy(hess_ref.at[:, cols], hess.at[:, cols], sems.at[c]))
        copies[-1].start()
    for c in range(chunks):
        copies[c].wait()
        cols = slice(c * width, (c + 1) * width)
        h = hess[:, cols]
        high = h.astype(BF16)
        high_ref[:, cols] = high
        low_ref[:, cols] = (h - high.astype(F32)).astype(BF16)


def split(hess_inv, after):
    chunks = 4
    return pl.pallas_call(
        functools.partial(split_kernel, chunks),
        out_shape=[pltpu.VMEM(hess_inv.shape, BF16)] * 2,
        in_specs=[HBM, VMEM],
        out_specs=[VMEM] * 2,
        scratch_shapes=[
            pltpu.VMEM(hess_inv.shape, F32),
            pltpu.SemaphoreType.DMA((chunks,)),
        ],
        compiler_params=pltpu.CompilerParams(vmem_limit_bytes=20 * 2**20),
        name="split",
    )(in_hbm(hess_inv), after)


def prepare_kernel(tokens, qlen, starts, *refs):
    pieces, (grads_ref, tok) = refs[:-2], refs[-2:]
    first = 0
    for piece, start in zip(pieces, starts):
        for part in range(piece.shape[0]):
            tok[first : first + tokens, :] = piece[part, start : start + tokens, :]
            first += tokens
    build(tok, qlen, grads_ref)


def prepare(tokens, qlen, coords, starts, *pieces):
    total = sum(piece.shape[0] for piece in pieces) * tokens
    rows = -(-total // (2 * GROUP)) * (2 * GROUP) // qlen
    return pl.pallas_call(
        functools.partial(prepare_kernel, tokens, qlen, starts),
        out_shape=pltpu.VMEM((rows, coords), BF16),
        in_specs=[VMEM] * len(pieces),
        out_specs=VMEM,
        scratch_shapes=[pltpu.VMEM((total, pieces[0].shape[2]), BF16)],
        compiler_params=pltpu.CompilerParams(vmem_limit_bytes=20 * 2**20),
        name="prepare",
    )(*pieces)


def score_kernel(number, each, slots, shares, rows_of, me_ref, *refs):
    pieces, refs = refs[: len(slots)], refs[len(slots) :]
    made_refs, (high_ref, low_ref, out_ref, train) = refs[: len(rows_of)], refs[len(rows_of) :]
    me = me_ref[0]
    block = high_ref.shape[0]
    n, tile, lanes = train.shape
    queries = n * each
    local = block // lanes

    for piece, froms, (first, second) in zip(pieces, slots, shares):
        for part, slot in enumerate(froms):
            both = piece[part, first : first + 2 * tile, :].astype(F32)
            train[me ^ slot] = both[tile:] if second else both[:tile]
    grads = jnp.concatenate([ref[...] for ref in made_refs], axis=0)
    precond = dot_nt(high_ref[...], grads) + dot_nt(low_ref[...], grads)
    row, col = iota((grads.shape[0], queries), 0), iota((grads.shape[0], queries), 1)
    place = jnp.full(row.shape, -1, jnp.int32)
    first = 0
    for ref, froms in zip(made_refs, rows_of):
        for i, slot in enumerate(froms):
            at = row - (first + i * each)
            place = jnp.where((at >= 0) & (at < each), (me ^ slot) * each + at, place)
        first += ref.shape[0]
    order = place == col
    precond = dot(precond.astype(BF16), order.astype(BF16)).astype(BF16)

    cols = pl.ds(pl.multiple_of(me * block, block), block)
    square = dot(jnp.concatenate([ref[:, cols] for ref in made_refs], axis=0), precond)
    self_inf = jnp.sum(jnp.where(order, square, 0.0), axis=0, keepdims=True)

    rows = n * tile
    t = train[...].reshape(rows, lanes)
    where = iota((rows, lanes), 0) % tile // number
    wide = jnp.concatenate(
        [jnp.where(where == j, t, 0.0).astype(BF16) for j in range(local)], axis=1
    )
    parts = dot(wide, precond)
    raw = parts
    for j in range(1, local):
        raw = raw + pltpu.roll(parts, rows - j * number, 0)
    raw = jnp.where(iota((rows, queries), 0) % tile < number, raw, self_inf)
    out_ref[...] = jnp.zeros_like(out_ref)
    out_ref[:, :queries] = raw


def score(me, number, each, pieces, slots, shares, made, rows_of, high, low):
    block = high.shape[0]
    lanes = pieces[0].shape[2]
    tile = block // lanes * number
    n = sum(map(len, slots))
    queries = n * each
    padded = -(-queries // 128) * 128
    return pl.pallas_call(
        functools.partial(score_kernel, number, each, slots, shares, rows_of),
        out_shape=pltpu.VMEM((n * tile, padded), F32),
        in_specs=[pl.BlockSpec(memory_space=pltpu.SMEM)] + [VMEM] * (len(pieces) + len(made) + 2),
        out_specs=VMEM,
        scratch_shapes=[pltpu.VMEM((n, tile, lanes), F32)],
        compiler_params=pltpu.CompilerParams(vmem_limit_bytes=20 * 2**20),
        name="score",
    )(me, *pieces, *made, high, low)


def finish_kernel(number, parts_ref, out_ref):
    total = jnp.sum(parts_ref[...], axis=0)
    queries = out_ref.shape[1]
    self_inf = total[number : number + 1, :queries]
    out_ref[...] = total[:number, :queries] / jnp.sqrt(self_inf)


def swap(x, k, n):
    return lax.ppermute(x, "dp", [(i, i ^ k) for i in range(n)])


def fast(n, train_hidden, train_cot, query_hidden, query_cot, proj_in, proj_out, hess_inv):
    number, qlen = train_hidden.shape[0], query_hidden.shape[1]
    tokens = query_hidden.shape[0] * qlen
    queries = n * query_hidden.shape[0]
    planes = n // INNER
    me = lax.axis_index("dp").astype(jnp.int32).reshape(1)
    messages = project(
        me, planes, train_hidden, train_cot, query_hidden, query_cot, proj_in, proj_out
    )
    coords = hess_inv.shape[1]
    others = [INNER * k for k in range(planes - 1, 0, -1)]
    far = [swap(messages[slot // INNER], slot, n) for slot in others]
    edge = (messages[0].shape[0] - tokens) // 2
    own_two = swap(messages[0][edge:], 2, n)
    by_plane = jnp.stack([messages[0]] + far)
    by_plane_one = swap(by_plane[:, :-edge], 1, n)
    by_two = jnp.concatenate([own_two[None], swap(jnp.stack(far)[:, edge:], 2, n)], axis=0)
    high, low = split(hess_inv, by_plane)
    made = [prepare(tokens, qlen, coords, [edge, edge], by_plane, by_plane_one)]
    by_two, high, low = lax.optimization_barrier((by_two, high, low))
    by_two_one = swap(by_two, 1, n)
    made += [prepare(tokens, qlen, coords, [0], piece) for piece in (by_two, by_two_one)]
    slots = [[first ^ slot for slot in [0] + others] for first in (0, 1, 2, 3)]
    rows_of = [slots[0] + slots[1], slots[2], slots[3]]
    pieces = [by_plane, by_plane_one, by_two, by_two_one]
    shares = [(0, False), (0, True), (tokens, True), (tokens, False)]
    each = tokens // qlen
    parts = score(me, number, each, pieces, slots, shares, made, rows_of, high, low)
    parts = parts.reshape(n, -1, parts.shape[1])
    parts = lax.all_to_all(parts, "dp", 0, 0, tiled=True)
    return pl.pallas_call(
        functools.partial(finish_kernel, number),
        out_shape=jax.ShapeDtypeStruct((number, queries), F32),
        in_specs=[VMEM],
        out_specs=VMEM,
        compiler_params=pltpu.CompilerParams(vmem_limit_bytes=4 * 2**20),
        name="finish",
    )(pltpu.with_memory_space_constraint(parts, pltpu.VMEM))


def suits(n, args):
    train_hidden, _, query_hidden, _, proj_in, _, hess_inv = args
    number, qlen = train_hidden.shape[0], query_hidden.shape[1]
    tokens = query_hidden.shape[0] * qlen
    lanes = 2 * proj_in.shape[0]
    block = hess_inv.shape[0]
    planes = n // INNER
    return (
        n % INNER == 0
        and planes > 1
        and planes & (planes - 1) == 0
        and lanes == 128
        and block % lanes == 0
        and block // lanes * number == 8
        and tokens % 16 == 0
        and GROUP == 8 * qlen
        and planes * tokens % GROUP == 0
        and 2 * planes * tokens % (2 * GROUP) == 0
    )


def on_device(n, *args):
    return fast(n, *args) if suits(n, args) else general(*args)


def solution(mesh):
    n = mesh.shape["dp"]
    in_specs = (
        P(("groups", "dp"), None, None),
        P(("groups", "dp"), None, None),
        P(("groups", "dp"), None, None),
        P(("groups", "dp"), None, None),
        P(),
        P(),
        P(("groups", "dp"), None),
    )
    out_specs = P(("groups", "dp"), None)
    return jax.shard_map(
        functools.partial(on_device, n),
        mesh=mesh,
        in_specs=in_specs,
        out_specs=out_specs,
        check_vma=False,
    )
```

```python
import functools

import jax
import jax.numpy as jnp
from jax import lax
from jax.experimental import pallas as pl
from jax.experimental.pallas import tpu as pltpu
from jax.sharding import PartitionSpec as P

F32, BF16 = jnp.float32, jnp.bfloat16
NT = (((1,), (1,)), ((), ()))
VMEM = pl.BlockSpec(memory_space=pltpu.VMEM)
HBM = pl.BlockSpec(memory_space=pltpu.HBM)
INNER = 4
GROUP = 128


def dot(a, b):
    return jnp.dot(a, b, preferred_element_type=F32)


def dot_nt(a, b):
    return lax.dot_general(a, b, NT, preferred_element_type=F32)


def in_hbm(x):
    return pltpu.with_memory_space_constraint(x, pltpu.HBM)


def iota(shape, dim):
    return lax.broadcasted_iota(jnp.int32, shape, dim)


def example_grads(hidden, cotangent, proj_in, proj_out):
    number, length, inner = hidden.shape
    outer_width = cotangent.shape[2]
    rank = proj_in.shape[0]
    inputs = jnp.dot(
        hidden.reshape(number * length, inner), proj_in.T, preferred_element_type=jnp.float32
    ).astype(jnp.bfloat16)
    outputs = jnp.dot(
        cotangent.reshape(number * length, outer_width),
        proj_out.T,
        preferred_element_type=jnp.float32,
    ).astype(jnp.bfloat16)
    inputs = inputs.reshape(number, length, rank)
    outputs = outputs.reshape(number, length, rank)
    summed = jnp.einsum("sto,sti->soi", outputs, inputs, preferred_element_type=jnp.float32) * (
        1.0 / length
    )
    return summed.astype(jnp.bfloat16).reshape(number, rank * rank)


def general(train_hidden, train_cot, query_hidden, query_cot, proj_in, proj_out, hess_inv):
    train_grads = example_grads(train_hidden, train_cot, proj_in, proj_out)
    query_grads = example_grads(query_hidden, query_cot, proj_in, proj_out)
    full_query = lax.all_gather(query_grads, "dp", axis=0, tiled=True).astype(jnp.float32)
    product = jnp.dot(full_query, hess_inv.T, precision=lax.Precision.HIGHEST)
    full_precond = lax.all_gather(product.astype(jnp.bfloat16), "dp", axis=1, tiled=True)
    self_inf = jnp.sum(full_query * full_precond.astype(jnp.float32), axis=1)
    raw = jnp.dot(train_grads, full_precond.T, preferred_element_type=jnp.float32)
    return raw / jnp.sqrt(self_inf)[None, :]


def project_kernel(
    planes, number, length, widths, me_ref, th_ref, tc_ref, qh_ref, qc_ref, pi_ref, po_ref, *rest
):
    outs, (th, tc, qh, qc, pi, po, grads, sems) = rest[:planes], rest[planes:]
    inner = th.shape[1]
    rank = pi.shape[0]
    tokens = th.shape[0]
    queries = qh.shape[0]

    copies = []

    def load(*pairs):
        group = []
        for src, dst in pairs:
            group.append(pltpu.make_async_copy(src, dst, sems.at[sum(map(len, copies)) + len(group)]))
            group[-1].start()
        copies.append(group)

    def arrived():
        for copy in copies.pop(0):
            copy.wait()

    parts = [slice(sum(widths[:c]), sum(widths[: c + 1])) for c in range(len(widths))]
    for c, cols in enumerate(parts):
        load(
            (pi_ref.at[:, cols], pi.at[:, cols]),
            (th_ref.at[:, cols], th.at[:, cols]),
            (qh_ref.at[:, cols], qh.at[:, cols]),
        )
        if c == 0:
            load((po_ref, po), (tc_ref, tc), (qc_ref, qc))

    rows = rank // 2 * number
    t_in = jnp.zeros((tokens, rank), F32)
    q_in = jnp.zeros((queries, rank), F32)
    for c, cols in enumerate(parts):
        arrived()
        middle = (cols.start + cols.stop) // 2
        for some in (slice(cols.start, middle), slice(middle, cols.stop)):
            t_in += dot_nt(th[:, some], pi[:, some])
            q_in += dot_nt(qh[:, some], pi[:, some])
        if c == 0:
            arrived()
            q_out = dot_nt(qc[...], po[...])
            t_out = dot_nt(po[...], tc[...]).astype(BF16)

    row, col = iota((rows, tokens), 0), iota((rows, tokens), 1)
    own = row % number == col // length
    lefts = []
    for half in range(2):
        pick = iota((rows, rank), 1) == 2 * (iota((rows, rank), 0) // number) + half
        lefts.append(jnp.where(own, dot(pick.astype(BF16), t_out), 0.0).astype(BF16))

    spread = jnp.concatenate([t_in, t_in], axis=1).astype(BF16)
    lane = iota((tokens, 2 * rank), 1)
    total = jnp.zeros((rows, 2 * rank), F32)
    for half in range(2):
        right = jnp.where(lane // rank == half, spread, jnp.zeros_like(spread))
        total += dot(lefts[half], right)
    grads[...] = total * (1.0 / length)
    message = jnp.concatenate([q_in, q_out], axis=1).astype(BF16)

    plane, inner = me_ref[0] // INNER, me_ref[0] % INNER
    tile = rows // planes // INNER
    edge = 2 * tile
    for k in range(planes):
        shares = [
            grads[pl.ds(pl.multiple_of(((plane ^ k) * INNER + (inner ^ j)) * tile, tile), tile), :]
            for j in ((0, 1, 3, 2) if k == 0 else (1, 0, 2, 3))
        ]
        outs[k][:edge, :] = jnp.concatenate(shares[:2], axis=0).astype(BF16)
        outs[k][edge : edge + queries, :] = message
        outs[k][edge + queries :, :] = jnp.concatenate(shares[2:], axis=0).astype(BF16)


def project(me, planes, train_hidden, train_cot, query_hidden, query_cot, proj_in, proj_out):
    number, length, inner = train_hidden.shape
    width = train_cot.shape[2]
    rank = proj_in.shape[0]
    tokens, queries = number * length, query_hidden.shape[0] * query_hidden.shape[1]
    rows = rank // 2 * number
    widths = [2048, 4096, 4096, 4096]
    return pl.pallas_call(
        functools.partial(project_kernel, planes, number, length, widths),
        out_shape=[pltpu.VMEM((queries + rows // planes, 2 * rank), BF16)] * planes,
        in_specs=[pl.BlockSpec(memory_space=pltpu.SMEM)] + [HBM] * 6,
        out_specs=[VMEM] * planes,
        scratch_shapes=[
            pltpu.VMEM((tokens, inner), BF16),
            pltpu.VMEM((tokens, width), BF16),
            pltpu.VMEM((queries, inner), BF16),
            pltpu.VMEM((queries, width), BF16),
            pltpu.VMEM((rank, inner), BF16),
            pltpu.VMEM((rank, width), BF16),
            pltpu.VMEM((rows, 2 * rank), F32),
            pltpu.SemaphoreType.DMA((3 * len(widths) + 3,)),
        ],
        compiler_params=pltpu.CompilerParams(vmem_limit_bytes=20 * 2**20),
        name="project",
    )(
        me,
        in_hbm(train_hidden.reshape(tokens, inner)),
        in_hbm(train_cot.reshape(tokens, width)),
        in_hbm(query_hidden.reshape(queries, inner)),
        in_hbm(query_cot.reshape(queries, width)),
        in_hbm(proj_in),
        in_hbm(proj_out),
    )


def build(tok, qlen, grads):
    lanes = tok.shape[1]
    rank = lanes // 2
    pairs = rank // 2
    per = GROUP // qlen
    groups = tok.shape[0] // GROUP
    pick = (iota((rank, lanes), 1) == iota((rank, lanes), 0) + rank).astype(BF16)
    shift = (iota((lanes, lanes), 1) == iota((lanes, lanes), 0) + rank).astype(BF16)
    own = iota((per, GROUP), 1) // qlen == iota((per, GROUP), 0)
    every = tok[...]
    outs = dot_nt(pick, every)
    moved = dot(every, shift).astype(BF16)
    still = jnp.where(iota(every.shape, 1) < rank, every, jnp.zeros_like(every))
    made = []
    for g in range(groups):
        cols = slice(g * GROUP, (g + 1) * GROUP)
        left = [
            jnp.concatenate(
                [
                    jnp.where(own, jnp.broadcast_to(outs[o : o + 1, cols], own.shape), 0.0)
                    for o in range(half, rank, 2)
                ],
                axis=0,
            ).astype(BF16)
            for half in range(2)
        ]
        right = jnp.concatenate([still[cols], moved[cols]], axis=0)
        made.append(dot(jnp.concatenate(left, axis=1), right) * (1.0 / qlen))
    made += [jnp.zeros_like(made[0])] * (groups % 2)
    for g in range(0, groups, 2):
        for pair in range(pairs):
            rows = slice(pair * per, (pair + 1) * per)
            grads[g * per : (g + 2) * per, pair * lanes : (pair + 1) * lanes] = jnp.concatenate(
                [made[g][rows], made[g + 1][rows]], axis=0
            ).astype(BF16)


def split_kernel(chunks, hess_ref, after_ref, high_ref, low_ref, hess, sems):
    width = hess.shape[1] // chunks
    copies = []
    for c in range(chunks):
        cols = pl.ds(c * width, width)
        copies.append(pltpu.make_async_copy(hess_ref.at[:, cols], hess.at[:, cols], sems.at[c]))
        copies[-1].start()
    for c in range(chunks):
        copies[c].wait()
        cols = slice(c * width, (c + 1) * width)
        h = hess[:, cols]
        high = h.astype(BF16)
        high_ref[:, cols] = high
        low_ref[:, cols] = (h - high.astype(F32)).astype(BF16)


def split(hess_inv, after):
    chunks = 4
    return pl.pallas_call(
        functools.partial(split_kernel, chunks),
        out_shape=[pltpu.VMEM(hess_inv.shape, BF16)] * 2,
        in_specs=[HBM, VMEM],
        out_specs=[VMEM] * 2,
        scratch_shapes=[
            pltpu.VMEM(hess_inv.shape, F32),
            pltpu.SemaphoreType.DMA((chunks,)),
        ],
        compiler_params=pltpu.CompilerParams(vmem_limit_bytes=20 * 2**20),
        name="split",
    )(in_hbm(hess_inv), after)


def prepare_kernel(tokens, qlen, starts, *refs):
    pieces, (grads_ref, tok) = refs[:-2], refs[-2:]
    first = 0
    for piece, start in zip(pieces, starts):
        for part in range(piece.shape[0]):
            tok[first : first + tokens, :] = piece[part, start : start + tokens, :]
            first += tokens
    build(tok, qlen, grads_ref)


def prepare(tokens, qlen, coords, starts, *pieces):
    total = sum(piece.shape[0] for piece in pieces) * tokens
    rows = -(-total // (2 * GROUP)) * (2 * GROUP) // qlen
    return pl.pallas_call(
        functools.partial(prepare_kernel, tokens, qlen, starts),
        out_shape=pltpu.VMEM((rows, coords), BF16),
        in_specs=[VMEM] * len(pieces),
        out_specs=VMEM,
        scratch_shapes=[pltpu.VMEM((total, pieces[0].shape[2]), BF16)],
        compiler_params=pltpu.CompilerParams(vmem_limit_bytes=20 * 2**20),
        name="prepare",
    )(*pieces)


def score_kernel(number, each, slots, shares, rows_of, me_ref, *refs):
    pieces, refs = refs[: len(slots)], refs[len(slots) :]
    made_refs, (high_ref, low_ref, out_ref, train) = refs[: len(rows_of)], refs[len(rows_of) :]
    me = me_ref[0]
    block = high_ref.shape[0]
    n, tile, lanes = train.shape
    queries = n * each
    local = block // lanes

    for piece, froms, (first, second) in zip(pieces, slots, shares):
        for part, slot in enumerate(froms):
            both = piece[part, first : first + 2 * tile, :].astype(F32)
            train[me ^ slot] = both[tile:] if second else both[:tile]
    grads = jnp.concatenate([ref[...] for ref in made_refs], axis=0)
    precond = dot_nt(high_ref[...], grads) + dot_nt(low_ref[...], grads)
    row, col = iota((grads.shape[0], queries), 0), iota((grads.shape[0], queries), 1)
    place = jnp.full(row.shape, -1, jnp.int32)
    first = 0
    for ref, froms in zip(made_refs, rows_of):
        for i, slot in enumerate(froms):
            at = row - (first + i * each)
            place = jnp.where((at >= 0) & (at < each), (me ^ slot) * each + at, place)
        first += ref.shape[0]
    order = place == col
    precond = dot(precond.astype(BF16), order.astype(BF16)).astype(BF16)

    cols = pl.ds(pl.multiple_of(me * block, block), block)
    square = dot(jnp.concatenate([ref[:, cols] for ref in made_refs], axis=0), precond)
    self_inf = jnp.sum(jnp.where(order, square, 0.0), axis=0, keepdims=True)

    rows = n * tile
    t = train[...].reshape(rows, lanes)
    where = iota((rows, lanes), 0) % tile // number
    wide = jnp.concatenate(
        [jnp.where(where == j, t, 0.0).astype(BF16) for j in range(local)], axis=1
    )
    parts = dot(wide, precond)
    raw = parts
    for j in range(1, local):
        raw = raw + pltpu.roll(parts, rows - j * number, 0)
    raw = jnp.where(iota((rows, queries), 0) % tile < number, raw, self_inf)
    out_ref[...] = jnp.zeros_like(out_ref)
    out_ref[:, :queries] = raw


def score(me, number, each, pieces, slots, shares, made, rows_of, high, low):
    block = high.shape[0]
    lanes = pieces[0].shape[2]
    tile = block // lanes * number
    n = sum(map(len, slots))
    queries = n * each
    padded = -(-queries // 128) * 128
    return pl.pallas_call(
        functools.partial(score_kernel, number, each, slots, shares, rows_of),
        out_shape=pltpu.VMEM((n * tile, padded), F32),
        in_specs=[pl.BlockSpec(memory_space=pltpu.SMEM)] + [VMEM] * (len(pieces) + len(made) + 2),
        out_specs=VMEM,
        scratch_shapes=[pltpu.VMEM((n, tile, lanes), F32)],
        compiler_params=pltpu.CompilerParams(vmem_limit_bytes=20 * 2**20),
        name="score",
    )(me, *pieces, *made, high, low)


def finish_kernel(number, parts_ref, out_ref):
    total = jnp.sum(parts_ref[...], axis=0)
    queries = out_ref.shape[1]
    self_inf = total[number : number + 1, :queries]
    out_ref[...] = total[:number, :queries] / jnp.sqrt(self_inf)


def swap(x, k, n):
    return lax.ppermute(x, "dp", [(i, i ^ k) for i in range(n)])


def fast(n, train_hidden, train_cot, query_hidden, query_cot, proj_in, proj_out, hess_inv):
    number, qlen = train_hidden.shape[0], query_hidden.shape[1]
    tokens = query_hidden.shape[0] * qlen
    queries = n * query_hidden.shape[0]
    planes = n // INNER
    me = lax.axis_index("dp").astype(jnp.int32).reshape(1)
    messages = project(
        me, planes, train_hidden, train_cot, query_hidden, query_cot, proj_in, proj_out
    )
    coords = hess_inv.shape[1]
    others = [(INNER * k) ^ 1 for k in range(planes - 1, 0, -1)]
    far = [swap(messages[slot // INNER], slot, n) for slot in others]
    edge = (messages[0].shape[0] - tokens) // 2
    by_plane = [messages[0]] + far
    halves = by_plane[: planes // 2], by_plane[planes // 2 :]
    by_two = jnp.concatenate([swap(jnp.stack(half)[:, edge:], 3, n) for half in halves], axis=0)
    by_plane = jnp.stack(by_plane)
    by_plane_one = swap(by_plane[:, :-edge], 1, n)
    high, low = split(hess_inv, by_plane)
    made = prepare(tokens, qlen, coords, [edge], by_plane)
    by_two, high, low, made = lax.optimization_barrier((by_two, high, low, made))
    by_two_one = swap(by_two, 1, n)
    made = [
        made,
        prepare(tokens, qlen, coords, [edge, 0], by_plane_one, by_two),
        prepare(tokens, qlen, coords, [0], by_two_one),
    ]
    slots = [[first ^ slot for slot in [0] + others] for first in (0, 1, 3, 2)]
    rows_of = [slots[0], slots[1] + slots[2], slots[3]]
    pieces = [by_plane, by_plane_one, by_two, by_two_one]
    shares = [(0, False), (0, True), (tokens, False), (tokens, True)]
    each = tokens // qlen
    parts = score(me, number, each, pieces, slots, shares, made, rows_of, high, low)
    parts = parts.reshape(n, -1, parts.shape[1])
    parts = lax.all_to_all(parts, "dp", 0, 0, tiled=True)
    return pl.pallas_call(
        functools.partial(finish_kernel, number),
        out_shape=jax.ShapeDtypeStruct((number, queries), F32),
        in_specs=[VMEM],
        out_specs=VMEM,
        compiler_params=pltpu.CompilerParams(vmem_limit_bytes=4 * 2**20),
        name="finish",
    )(pltpu.with_memory_space_constraint(parts, pltpu.VMEM))


def suits(n, args):
    train_hidden, _, query_hidden, _, proj_in, _, hess_inv = args
    number, qlen = train_hidden.shape[0], query_hidden.shape[1]
    tokens = query_hidden.shape[0] * qlen
    lanes = 2 * proj_in.shape[0]
    block = hess_inv.shape[0]
    planes = n // INNER
    return (
        n % INNER == 0
        and planes > 1
        and planes & (planes - 1) == 0
        and lanes == 128
        and block % lanes == 0
        and block // lanes * number == 8
        and tokens % 16 == 0
        and GROUP == 8 * qlen
        and planes * tokens % GROUP == 0
        and 2 * planes * tokens % (2 * GROUP) == 0
    )


def on_device(n, *args):
    return fast(n, *args) if suits(n, args) else general(*args)


def solution(mesh):
    n = mesh.shape["dp"]
    in_specs = (
        P(("groups", "dp"), None, None),
        P(("groups", "dp"), None, None),
        P(("groups", "dp"), None, None),
        P(("groups", "dp"), None, None),
        P(),
        P(),
        P(("groups", "dp"), None),
    )
    out_specs = P(("groups", "dp"), None)
    return jax.shard_map(
        functools.partial(on_device, n),
        mesh=mesh,
        in_specs=in_specs,
        out_specs=out_specs,
        check_vma=False,
    )
```

```python
import functools

import jax
import jax.numpy as jnp
from jax import lax
from jax.experimental import pallas as pl
from jax.experimental.pallas import tpu as pltpu
from jax.sharding import PartitionSpec as P

F32, BF16 = jnp.float32, jnp.bfloat16
NT = (((1,), (1,)), ((), ()))
VMEM = pl.BlockSpec(memory_space=pltpu.VMEM)
HBM = pl.BlockSpec(memory_space=pltpu.HBM)
INNER = 4
GROUP = 128


def dot(a, b):
    return jnp.dot(a, b, preferred_element_type=F32)


def dot_nt(a, b):
    return lax.dot_general(a, b, NT, preferred_element_type=F32)


def in_hbm(x):
    return pltpu.with_memory_space_constraint(x, pltpu.HBM)


def iota(shape, dim):
    return lax.broadcasted_iota(jnp.int32, shape, dim)


def example_grads(hidden, cotangent, proj_in, proj_out):
    number, length, inner = hidden.shape
    outer_width = cotangent.shape[2]
    rank = proj_in.shape[0]
    inputs = jnp.dot(
        hidden.reshape(number * length, inner), proj_in.T, preferred_element_type=jnp.float32
    ).astype(jnp.bfloat16)
    outputs = jnp.dot(
        cotangent.reshape(number * length, outer_width),
        proj_out.T,
        preferred_element_type=jnp.float32,
    ).astype(jnp.bfloat16)
    inputs = inputs.reshape(number, length, rank)
    outputs = outputs.reshape(number, length, rank)
    summed = jnp.einsum("sto,sti->soi", outputs, inputs, preferred_element_type=jnp.float32) * (
        1.0 / length
    )
    return summed.astype(jnp.bfloat16).reshape(number, rank * rank)


def general(train_hidden, train_cot, query_hidden, query_cot, proj_in, proj_out, hess_inv):
    train_grads = example_grads(train_hidden, train_cot, proj_in, proj_out)
    query_grads = example_grads(query_hidden, query_cot, proj_in, proj_out)
    full_query = lax.all_gather(query_grads, "dp", axis=0, tiled=True).astype(jnp.float32)
    product = jnp.dot(full_query, hess_inv.T, precision=lax.Precision.HIGHEST)
    full_precond = lax.all_gather(product.astype(jnp.bfloat16), "dp", axis=1, tiled=True)
    self_inf = jnp.sum(full_query * full_precond.astype(jnp.float32), axis=1)
    raw = jnp.dot(train_grads, full_precond.T, preferred_element_type=jnp.float32)
    return raw / jnp.sqrt(self_inf)[None, :]


def project_kernel(
    planes, number, length, widths, me_ref, th_ref, tc_ref, qh_ref, qc_ref, pi_ref, po_ref, *rest
):
    outs, (th, tc, qh, qc, pi, po, grads, sems) = rest[:planes], rest[planes:]
    inner = th.shape[1]
    rank = pi.shape[0]
    tokens = th.shape[0]
    queries = qh.shape[0]

    copies = []

    def load(*pairs):
        group = []
        for src, dst in pairs:
            group.append(pltpu.make_async_copy(src, dst, sems.at[sum(map(len, copies)) + len(group)]))
            group[-1].start()
        copies.append(group)

    def arrived():
        for copy in copies.pop(0):
            copy.wait()

    parts = [slice(sum(widths[:c]), sum(widths[: c + 1])) for c in range(len(widths))]
    for c, cols in enumerate(parts):
        load(
            (pi_ref.at[:, cols], pi.at[:, cols]),
            (th_ref.at[:, cols], th.at[:, cols]),
            (qh_ref.at[:, cols], qh.at[:, cols]),
        )
        if c == 0:
            load((po_ref, po), (tc_ref, tc), (qc_ref, qc))

    rows = rank // 2 * number
    t_in = jnp.zeros((tokens, rank), F32)
    q_in = jnp.zeros((queries, rank), F32)
    for c, cols in enumerate(parts):
        arrived()
        middle = (cols.start + cols.stop) // 2
        for some in (slice(cols.start, middle), slice(middle, cols.stop)):
            t_in += dot_nt(th[:, some], pi[:, some])
            q_in += dot_nt(qh[:, some], pi[:, some])
        if c == 0:
            arrived()
            q_out = dot_nt(qc[...], po[...])
            t_out = dot_nt(po[...], tc[...]).astype(BF16)

    row, col = iota((rows, tokens), 0), iota((rows, tokens), 1)
    own = row % number == col // length
    lefts = []
    for half in range(2):
        pick = iota((rows, rank), 1) == 2 * (iota((rows, rank), 0) // number) + half
        lefts.append(jnp.where(own, dot(pick.astype(BF16), t_out), 0.0).astype(BF16))

    spread = jnp.concatenate([t_in, t_in], axis=1).astype(BF16)
    lane = iota((tokens, 2 * rank), 1)
    total = jnp.zeros((rows, 2 * rank), F32)
    for half in range(2):
        right = jnp.where(lane // rank == half, spread, jnp.zeros_like(spread))
        total += dot(lefts[half], right)
    grads[...] = total * (1.0 / length)
    message = jnp.concatenate([q_in, q_out], axis=1).astype(BF16)

    plane, inner = me_ref[0] // INNER, me_ref[0] % INNER
    tile = rows // planes // INNER
    edge = 2 * tile
    for k in range(planes):
        shares = [
            grads[pl.ds(pl.multiple_of(((plane ^ k) * INNER + (inner ^ j)) * tile, tile), tile), :]
            for j in ((0, 1, 3, 2) if k == 0 else (1, 0, 2, 3))
        ]
        outs[k][:edge, :] = jnp.concatenate(shares[:2], axis=0).astype(BF16)
        outs[k][edge : edge + queries, :] = message
        outs[k][edge + queries :, :] = jnp.concatenate(shares[2:], axis=0).astype(BF16)


def project(me, planes, train_hidden, train_cot, query_hidden, query_cot, proj_in, proj_out):
    number, length, inner = train_hidden.shape
    width = train_cot.shape[2]
    rank = proj_in.shape[0]
    tokens, queries = number * length, query_hidden.shape[0] * query_hidden.shape[1]
    rows = rank // 2 * number
    widths = [2048, 4096, 4096, 4096]
    return pl.pallas_call(
        functools.partial(project_kernel, planes, number, length, widths),
        out_shape=[pltpu.VMEM((queries + rows // planes, 2 * rank), BF16)] * planes,
        in_specs=[pl.BlockSpec(memory_space=pltpu.SMEM)] + [HBM] * 6,
        out_specs=[VMEM] * planes,
        scratch_shapes=[
            pltpu.VMEM((tokens, inner), BF16),
            pltpu.VMEM((tokens, width), BF16),
            pltpu.VMEM((queries, inner), BF16),
            pltpu.VMEM((queries, width), BF16),
            pltpu.VMEM((rank, inner), BF16),
            pltpu.VMEM((rank, width), BF16),
            pltpu.VMEM((rows, 2 * rank), F32),
            pltpu.SemaphoreType.DMA((3 * len(widths) + 3,)),
        ],
        compiler_params=pltpu.CompilerParams(vmem_limit_bytes=20 * 2**20),
        name="project",
    )(
        me,
        in_hbm(train_hidden.reshape(tokens, inner)),
        in_hbm(train_cot.reshape(tokens, width)),
        in_hbm(query_hidden.reshape(queries, inner)),
        in_hbm(query_cot.reshape(queries, width)),
        in_hbm(proj_in),
        in_hbm(proj_out),
    )


def build(tok, qlen, grads):
    lanes = tok.shape[1]
    rank = lanes // 2
    pairs = rank // 2
    per = GROUP // qlen
    groups = tok.shape[0] // GROUP
    pick = (iota((rank, lanes), 1) == iota((rank, lanes), 0) + rank).astype(BF16)
    shift = (iota((lanes, lanes), 1) == iota((lanes, lanes), 0) + rank).astype(BF16)
    own = iota((per, GROUP), 1) // qlen == iota((per, GROUP), 0)
    every = tok[...]
    outs = dot_nt(pick, every)
    moved = dot(every, shift).astype(BF16)
    still = jnp.where(iota(every.shape, 1) < rank, every, jnp.zeros_like(every))
    made = []
    for g in range(groups):
        cols = slice(g * GROUP, (g + 1) * GROUP)
        left = [
            jnp.concatenate(
                [
                    jnp.where(own, jnp.broadcast_to(outs[o : o + 1, cols], own.shape), 0.0)
                    for o in range(half, rank, 2)
                ],
                axis=0,
            ).astype(BF16)
            for half in range(2)
        ]
        right = jnp.concatenate([still[cols], moved[cols]], axis=0)
        made.append(dot(jnp.concatenate(left, axis=1), right) * (1.0 / qlen))
    made += [jnp.zeros_like(made[0])] * (groups % 2)
    for g in range(0, groups, 2):
        for pair in range(pairs):
            rows = slice(pair * per, (pair + 1) * per)
            grads[g * per : (g + 2) * per, pair * lanes : (pair + 1) * lanes] = jnp.concatenate(
                [made[g][rows], made[g + 1][rows]], axis=0
            ).astype(BF16)


def split_kernel(chunks, hess_ref, after_ref, high_ref, low_ref, hess, sems):
    width = hess.shape[1] // chunks
    copies = []
    for c in range(chunks):
        cols = pl.ds(c * width, width)
        copies.append(pltpu.make_async_copy(hess_ref.at[:, cols], hess.at[:, cols], sems.at[c]))
        copies[-1].start()
    for c in range(chunks):
        copies[c].wait()
        cols = slice(c * width, (c + 1) * width)
        h = hess[:, cols]
        high = h.astype(BF16)
        high_ref[:, cols] = high
        low_ref[:, cols] = (h - high.astype(F32)).astype(BF16)


def split(hess_inv, after):
    chunks = 4
    return pl.pallas_call(
        functools.partial(split_kernel, chunks),
        out_shape=[pltpu.VMEM(hess_inv.shape, BF16)] * 2,
        in_specs=[HBM, VMEM],
        out_specs=[VMEM] * 2,
        scratch_shapes=[
            pltpu.VMEM(hess_inv.shape, F32),
            pltpu.SemaphoreType.DMA((chunks,)),
        ],
        compiler_params=pltpu.CompilerParams(vmem_limit_bytes=20 * 2**20),
        name="split",
    )(in_hbm(hess_inv), after)


def prepare_kernel(tokens, qlen, starts, *refs):
    pieces, (grads_ref, tok) = refs[:-2], refs[-2:]
    first = 0
    for piece, start in zip(pieces, starts):
        for part in range(piece.shape[0]):
            tok[first : first + tokens, :] = piece[part, start : start + tokens, :]
            first += tokens
    build(tok, qlen, grads_ref)


def prepare(tokens, qlen, coords, starts, *pieces):
    total = sum(piece.shape[0] for piece in pieces) * tokens
    rows = -(-total // (2 * GROUP)) * (2 * GROUP) // qlen
    return pl.pallas_call(
        functools.partial(prepare_kernel, tokens, qlen, starts),
        out_shape=pltpu.VMEM((rows, coords), BF16),
        in_specs=[VMEM] * len(pieces),
        out_specs=VMEM,
        scratch_shapes=[pltpu.VMEM((total, pieces[0].shape[2]), BF16)],
        compiler_params=pltpu.CompilerParams(vmem_limit_bytes=20 * 2**20),
        name="prepare",
    )(*pieces)


def score_kernel(number, each, slots, shares, rows_of, me_ref, *refs):
    pieces, refs = refs[: len(slots)], refs[len(slots) :]
    made_refs, (high_ref, low_ref, out_ref, train) = refs[: len(rows_of)], refs[len(rows_of) :]
    me = me_ref[0]
    block = high_ref.shape[0]
    n, tile, lanes = train.shape
    queries = n * each
    local = block // lanes

    for piece, froms, (first, second) in zip(pieces, slots, shares):
        for part, slot in enumerate(froms):
            both = piece[part, first : first + 2 * tile, :].astype(F32)
            train[me ^ slot] = both[tile:] if second else both[:tile]
    grads = jnp.concatenate([ref[...] for ref in made_refs], axis=0)
    precond = dot_nt(high_ref[...], grads) + dot_nt(low_ref[...], grads)
    row, col = iota((grads.shape[0], queries), 0), iota((grads.shape[0], queries), 1)
    place = jnp.full(row.shape, -1, jnp.int32)
    first = 0
    for ref, froms in zip(made_refs, rows_of):
        for i, slot in enumerate(froms):
            at = row - (first + i * each)
            place = jnp.where((at >= 0) & (at < each), (me ^ slot) * each + at, place)
        first += ref.shape[0]
    order = place == col
    precond = dot(precond.astype(BF16), order.astype(BF16)).astype(BF16)

    cols = pl.ds(pl.multiple_of(me * block, block), block)
    square = dot(jnp.concatenate([ref[:, cols] for ref in made_refs], axis=0), precond)
    self_inf = jnp.sum(jnp.where(order, square, 0.0), axis=0, keepdims=True)

    rows = n * tile
    t = train[...].reshape(rows, lanes)
    where = iota((rows, lanes), 0) % tile // number
    wide = jnp.concatenate(
        [jnp.where(where == j, t, 0.0).astype(BF16) for j in range(local)], axis=1
    )
    parts = dot(wide, precond)
    raw = parts
    for j in range(1, local):
        raw = raw + pltpu.roll(parts, rows - j * number, 0)
    raw = jnp.where(iota((rows, queries), 0) % tile < number, raw, self_inf)
    out_ref[...] = jnp.zeros_like(out_ref)
    out_ref[:, :queries] = raw


def score(me, number, each, pieces, slots, shares, made, rows_of, high, low):
    block = high.shape[0]
    lanes = pieces[0].shape[2]
    tile = block // lanes * number
    n = sum(map(len, slots))
    queries = n * each
    padded = -(-queries // 128) * 128
    return pl.pallas_call(
        functools.partial(score_kernel, number, each, slots, shares, rows_of),
        out_shape=pltpu.VMEM((n * tile, padded), F32),
        in_specs=[pl.BlockSpec(memory_space=pltpu.SMEM)] + [VMEM] * (len(pieces) + len(made) + 2),
        out_specs=VMEM,
        scratch_shapes=[pltpu.VMEM((n, tile, lanes), F32)],
        compiler_params=pltpu.CompilerParams(vmem_limit_bytes=20 * 2**20),
        name="score",
    )(me, *pieces, *made, high, low)


def finish_kernel(number, parts_ref, out_ref):
    total = jnp.sum(parts_ref[...], axis=0)
    queries = out_ref.shape[1]
    self_inf = total[number : number + 1, :queries]
    out_ref[...] = total[:number, :queries] / jnp.sqrt(self_inf)


def swap(x, k, n):
    return lax.ppermute(x, "dp", [(i, i ^ k) for i in range(n)])


def fast(n, train_hidden, train_cot, query_hidden, query_cot, proj_in, proj_out, hess_inv):
    number, qlen = train_hidden.shape[0], query_hidden.shape[1]
    tokens = query_hidden.shape[0] * qlen
    queries = n * query_hidden.shape[0]
    planes = n // INNER
    me = lax.axis_index("dp").astype(jnp.int32).reshape(1)
    messages = project(
        me, planes, train_hidden, train_cot, query_hidden, query_cot, proj_in, proj_out
    )
    coords = hess_inv.shape[1]
    others = [(INNER * k) ^ 1 for k in range(planes - 1, 0, -1)]
    far = [swap(messages[slot // INNER], slot, n) for slot in others]
    edge = (messages[0].shape[0] - tokens) // 2
    by_plane = [messages[0]] + far
    near = swap(messages[1][edge:], others[-1] ^ 3, n)
    by_two = swap(jnp.stack(by_plane[:-1])[:, edge:], 3, n)
    by_two = jnp.concatenate([by_two, near[None]], axis=0)
    by_plane = jnp.stack(by_plane)
    by_plane_one = swap(by_plane[:, :-edge], 1, n)
    high, low = split(hess_inv, by_plane)
    made = prepare(tokens, qlen, coords, [edge], by_plane)
    by_two, high, low, made = lax.optimization_barrier((by_two, high, low, made))
    by_two_one = swap(by_two, 1, n)
    made = [
        made,
        prepare(tokens, qlen, coords, [edge, 0], by_plane_one, by_two),
        prepare(tokens, qlen, coords, [0], by_two_one),
    ]
    slots = [[first ^ slot for slot in [0] + others] for first in (0, 1, 3, 2)]
    rows_of = [slots[0], slots[1] + slots[2], slots[3]]
    pieces = [by_plane, by_plane_one, by_two, by_two_one]
    shares = [(0, False), (0, True), (tokens, False), (tokens, True)]
    each = tokens // qlen
    parts = score(me, number, each, pieces, slots, shares, made, rows_of, high, low)
    parts = parts.reshape(n, -1, parts.shape[1])
    parts = lax.all_to_all(parts, "dp", 0, 0, tiled=True)
    return pl.pallas_call(
        functools.partial(finish_kernel, number),
        out_shape=jax.ShapeDtypeStruct((number, queries), F32),
        in_specs=[VMEM],
        out_specs=VMEM,
        compiler_params=pltpu.CompilerParams(vmem_limit_bytes=4 * 2**20),
        name="finish",
    )(pltpu.with_memory_space_constraint(parts, pltpu.VMEM))


def suits(n, args):
    train_hidden, _, query_hidden, _, proj_in, _, hess_inv = args
    number, qlen = train_hidden.shape[0], query_hidden.shape[1]
    tokens = query_hidden.shape[0] * qlen
    lanes = 2 * proj_in.shape[0]
    block = hess_inv.shape[0]
    planes = n // INNER
    return (
        n % INNER == 0
        and planes > 1
        and planes & (planes - 1) == 0
        and lanes == 128
        and block % lanes == 0
        and block // lanes * number == 8
        and tokens % 16 == 0
        and GROUP == 8 * qlen
        and planes * tokens % GROUP == 0
        and 2 * planes * tokens % (2 * GROUP) == 0
    )


def on_device(n, *args):
    return fast(n, *args) if suits(n, args) else general(*args)


def solution(mesh):
    n = mesh.shape["dp"]
    in_specs = (
        P(("groups", "dp"), None, None),
        P(("groups", "dp"), None, None),
        P(("groups", "dp"), None, None),
        P(("groups", "dp"), None, None),
        P(),
        P(),
        P(("groups", "dp"), None),
    )
    out_specs = P(("groups", "dp"), None)
    return jax.shard_map(
        functools.partial(on_device, n),
        mesh=mesh,
        in_specs=in_specs,
        out_specs=out_specs,
        check_vma=False,
    )
```

```python
import functools

import jax
import jax.numpy as jnp
from jax import lax
from jax.experimental import pallas as pl
from jax.experimental.pallas import tpu as pltpu
from jax.sharding import PartitionSpec as P

F32, BF16 = jnp.float32, jnp.bfloat16
NT = (((1,), (1,)), ((), ()))
VMEM = pl.BlockSpec(memory_space=pltpu.VMEM)
HBM = pl.BlockSpec(memory_space=pltpu.HBM)
INNER = 4
GROUP = 128


def dot(a, b):
    return jnp.dot(a, b, preferred_element_type=F32)


def dot_nt(a, b):
    return lax.dot_general(a, b, NT, preferred_element_type=F32)


def in_hbm(x):
    return pltpu.with_memory_space_constraint(x, pltpu.HBM)


def iota(shape, dim):
    return lax.broadcasted_iota(jnp.int32, shape, dim)


def example_grads(hidden, cotangent, proj_in, proj_out):
    number, length, inner = hidden.shape
    outer_width = cotangent.shape[2]
    rank = proj_in.shape[0]
    inputs = jnp.dot(
        hidden.reshape(number * length, inner), proj_in.T, preferred_element_type=jnp.float32
    ).astype(jnp.bfloat16)
    outputs = jnp.dot(
        cotangent.reshape(number * length, outer_width),
        proj_out.T,
        preferred_element_type=jnp.float32,
    ).astype(jnp.bfloat16)
    inputs = inputs.reshape(number, length, rank)
    outputs = outputs.reshape(number, length, rank)
    summed = jnp.einsum("sto,sti->soi", outputs, inputs, preferred_element_type=jnp.float32) * (
        1.0 / length
    )
    return summed.astype(jnp.bfloat16).reshape(number, rank * rank)


def general(train_hidden, train_cot, query_hidden, query_cot, proj_in, proj_out, hess_inv):
    train_grads = example_grads(train_hidden, train_cot, proj_in, proj_out)
    query_grads = example_grads(query_hidden, query_cot, proj_in, proj_out)
    full_query = lax.all_gather(query_grads, "dp", axis=0, tiled=True).astype(jnp.float32)
    product = jnp.dot(full_query, hess_inv.T, precision=lax.Precision.HIGHEST)
    full_precond = lax.all_gather(product.astype(jnp.bfloat16), "dp", axis=1, tiled=True)
    self_inf = jnp.sum(full_query * full_precond.astype(jnp.float32), axis=1)
    raw = jnp.dot(train_grads, full_precond.T, preferred_element_type=jnp.float32)
    return raw / jnp.sqrt(self_inf)[None, :]


def project_kernel(
    planes, number, length, widths, me_ref, th_ref, tc_ref, qh_ref, qc_ref, pi_ref, po_ref, *rest
):
    outs, (th, tc, qh, qc, pi, po, grads, sems) = rest[:planes], rest[planes:]
    inner = th.shape[1]
    rank = pi.shape[0]
    tokens = th.shape[0]
    queries = qh.shape[0]

    copies = []

    def load(*pairs):
        group = []
        for src, dst in pairs:
            group.append(pltpu.make_async_copy(src, dst, sems.at[sum(map(len, copies)) + len(group)]))
            group[-1].start()
        copies.append(group)

    def arrived():
        for copy in copies.pop(0):
            copy.wait()

    parts = [slice(sum(widths[:c]), sum(widths[: c + 1])) for c in range(len(widths))]
    for c, cols in enumerate(parts):
        load(
            (pi_ref.at[:, cols], pi.at[:, cols]),
            (th_ref.at[:, cols], th.at[:, cols]),
            (qh_ref.at[:, cols], qh.at[:, cols]),
        )
        if c == 0:
            load((po_ref, po), (tc_ref, tc), (qc_ref, qc))

    rows = rank // 2 * number
    t_in = jnp.zeros((tokens, rank), F32)
    q_in = jnp.zeros((queries, rank), F32)
    for c, cols in enumerate(parts):
        arrived()
        middle = (cols.start + cols.stop) // 2
        for some in (slice(cols.start, middle), slice(middle, cols.stop)):
            t_in += dot_nt(th[:, some], pi[:, some])
            q_in += dot_nt(qh[:, some], pi[:, some])
        if c == 0:
            arrived()
            q_out = dot_nt(qc[...], po[...])
            t_out = dot_nt(po[...], tc[...]).astype(BF16)

    row, col = iota((rows, tokens), 0), iota((rows, tokens), 1)
    own = row % number == col // length
    lefts = []
    for half in range(2):
        pick = iota((rows, rank), 1) == 2 * (iota((rows, rank), 0) // number) + half
        lefts.append(jnp.where(own, dot(pick.astype(BF16), t_out), 0.0).astype(BF16))

    spread = jnp.concatenate([t_in, t_in], axis=1).astype(BF16)
    lane = iota((tokens, 2 * rank), 1)
    total = jnp.zeros((rows, 2 * rank), F32)
    for half in range(2):
        right = jnp.where(lane // rank == half, spread, jnp.zeros_like(spread))
        total += dot(lefts[half], right)
    grads[...] = total * (1.0 / length)
    message = jnp.concatenate([q_in, q_out], axis=1).astype(BF16)

    plane, inner = me_ref[0] // INNER, me_ref[0] % INNER
    tile = rows // planes // INNER
    edge = 2 * tile
    for k in range(planes):
        shares = [
            grads[pl.ds(pl.multiple_of(((plane ^ k) * INNER + (inner ^ j)) * tile, tile), tile), :]
            for j in ((0, 1, 3, 2) if k == 0 else (1, 0, 2, 3))
        ]
        outs[k][:edge, :] = jnp.concatenate(shares[:2], axis=0).astype(BF16)
        outs[k][edge : edge + queries, :] = message
        outs[k][edge + queries :, :] = jnp.concatenate(shares[2:], axis=0).astype(BF16)


def project(me, planes, train_hidden, train_cot, query_hidden, query_cot, proj_in, proj_out):
    number, length, inner = train_hidden.shape
    width = train_cot.shape[2]
    rank = proj_in.shape[0]
    tokens, queries = number * length, query_hidden.shape[0] * query_hidden.shape[1]
    rows = rank // 2 * number
    widths = [2048, 4096, 4096, 4096]
    return pl.pallas_call(
        functools.partial(project_kernel, planes, number, length, widths),
        out_shape=[pltpu.VMEM((queries + rows // planes, 2 * rank), BF16)] * planes,
        in_specs=[pl.BlockSpec(memory_space=pltpu.SMEM)] + [HBM] * 6,
        out_specs=[VMEM] * planes,
        scratch_shapes=[
            pltpu.VMEM((tokens, inner), BF16),
            pltpu.VMEM((tokens, width), BF16),
            pltpu.VMEM((queries, inner), BF16),
            pltpu.VMEM((queries, width), BF16),
            pltpu.VMEM((rank, inner), BF16),
            pltpu.VMEM((rank, width), BF16),
            pltpu.VMEM((rows, 2 * rank), F32),
            pltpu.SemaphoreType.DMA((3 * len(widths) + 3,)),
        ],
        compiler_params=pltpu.CompilerParams(vmem_limit_bytes=20 * 2**20),
        name="project",
    )(
        me,
        in_hbm(train_hidden.reshape(tokens, inner)),
        in_hbm(train_cot.reshape(tokens, width)),
        in_hbm(query_hidden.reshape(queries, inner)),
        in_hbm(query_cot.reshape(queries, width)),
        in_hbm(proj_in),
        in_hbm(proj_out),
    )


def build(tok, qlen, grads):
    lanes = tok.shape[1]
    rank = lanes // 2
    pairs = rank // 2
    per = GROUP // qlen
    groups = tok.shape[0] // GROUP
    pick = (iota((rank, lanes), 1) == iota((rank, lanes), 0) + rank).astype(BF16)
    shift = (iota((lanes, lanes), 1) == iota((lanes, lanes), 0) + rank).astype(BF16)
    own = iota((per, GROUP), 1) // qlen == iota((per, GROUP), 0)
    every = tok[...]
    outs = dot_nt(pick, every)
    moved = dot(every, shift).astype(BF16)
    still = jnp.where(iota(every.shape, 1) < rank, every, jnp.zeros_like(every))
    made = []
    for g in range(groups):
        cols = slice(g * GROUP, (g + 1) * GROUP)
        left = [
            jnp.concatenate(
                [
                    jnp.where(own, jnp.broadcast_to(outs[o : o + 1, cols], own.shape), 0.0)
                    for o in range(half, rank, 2)
                ],
                axis=0,
            ).astype(BF16)
            for half in range(2)
        ]
        right = jnp.concatenate([still[cols], moved[cols]], axis=0)
        made.append(dot(jnp.concatenate(left, axis=1), right) * (1.0 / qlen))
    made += [jnp.zeros_like(made[0])] * (groups % 2)
    for g in range(0, groups, 2):
        for pair in range(pairs):
            rows = slice(pair * per, (pair + 1) * per)
            grads[g * per : (g + 2) * per, pair * lanes : (pair + 1) * lanes] = jnp.concatenate(
                [made[g][rows], made[g + 1][rows]], axis=0
            ).astype(BF16)


def split_kernel(chunks, hess_ref, after_ref, high_ref, low_ref, hess, sems):
    width = hess.shape[1] // chunks
    copies = []
    for c in range(chunks):
        cols = pl.ds(c * width, width)
        copies.append(pltpu.make_async_copy(hess_ref.at[:, cols], hess.at[:, cols], sems.at[c]))
        copies[-1].start()
    for c in range(chunks):
        copies[c].wait()
        cols = slice(c * width, (c + 1) * width)
        h = hess[:, cols]
        high = h.astype(BF16)
        high_ref[:, cols] = high
        low_ref[:, cols] = (h - high.astype(F32)).astype(BF16)


def split(hess_inv, after):
    chunks = 4
    return pl.pallas_call(
        functools.partial(split_kernel, chunks),
        out_shape=[pltpu.VMEM(hess_inv.shape, BF16)] * 2,
        in_specs=[HBM, VMEM],
        out_specs=[VMEM] * 2,
        scratch_shapes=[
            pltpu.VMEM(hess_inv.shape, F32),
            pltpu.SemaphoreType.DMA((chunks,)),
        ],
        compiler_params=pltpu.CompilerParams(vmem_limit_bytes=20 * 2**20),
        name="split",
    )(in_hbm(hess_inv), after)


def prepare_kernel(tokens, qlen, starts, *refs):
    pieces, (grads_ref, tok) = refs[:-2], refs[-2:]
    first = 0
    for piece, start in zip(pieces, starts):
        for part in range(piece.shape[0]):
            tok[first : first + tokens, :] = piece[part, start : start + tokens, :]
            first += tokens
    build(tok, qlen, grads_ref)


def prepare(tokens, qlen, coords, starts, *pieces):
    total = sum(piece.shape[0] for piece in pieces) * tokens
    rows = -(-total // (2 * GROUP)) * (2 * GROUP) // qlen
    return pl.pallas_call(
        functools.partial(prepare_kernel, tokens, qlen, starts),
        out_shape=pltpu.VMEM((rows, coords), BF16),
        in_specs=[VMEM] * len(pieces),
        out_specs=VMEM,
        scratch_shapes=[pltpu.VMEM((total, pieces[0].shape[2]), BF16)],
        compiler_params=pltpu.CompilerParams(vmem_limit_bytes=20 * 2**20),
        name="prepare",
    )(*pieces)


def score_kernel(number, each, slots, shares, rows_of, me_ref, *refs):
    pieces, refs = refs[: len(slots)], refs[len(slots) :]
    made_refs, (high_ref, low_ref, out_ref, train) = refs[: len(rows_of)], refs[len(rows_of) :]
    me = me_ref[0]
    block = high_ref.shape[0]
    n, tile, lanes = train.shape
    queries = n * each
    local = block // lanes

    for piece, froms, (first, second) in zip(pieces, slots, shares):
        for part, slot in enumerate(froms):
            both = piece[part, first : first + 2 * tile, :].astype(F32)
            train[me ^ slot] = both[tile:] if second else both[:tile]
    grads = jnp.concatenate([ref[...] for ref in made_refs], axis=0)
    precond = dot_nt(high_ref[...], grads) + dot_nt(low_ref[...], grads)
    row, col = iota((grads.shape[0], queries), 0), iota((grads.shape[0], queries), 1)
    place = jnp.full(row.shape, -1, jnp.int32)
    first = 0
    for ref, froms in zip(made_refs, rows_of):
        for i, slot in enumerate(froms):
            at = row - (first + i * each)
            place = jnp.where((at >= 0) & (at < each), (me ^ slot) * each + at, place)
        first += ref.shape[0]
    order = place == col
    precond = dot(precond.astype(BF16), order.astype(BF16)).astype(BF16)

    cols = pl.ds(pl.multiple_of(me * block, block), block)
    square = dot(jnp.concatenate([ref[:, cols] for ref in made_refs], axis=0), precond)
    self_inf = jnp.sum(jnp.where(order, square, 0.0), axis=0, keepdims=True)

    rows = n * tile
    t = train[...].reshape(rows, lanes)
    where = iota((rows, lanes), 0) % tile // number
    wide = jnp.concatenate(
        [jnp.where(where == j, t, 0.0).astype(BF16) for j in range(local)], axis=1
    )
    parts = dot(wide, precond)
    raw = parts
    for j in range(1, local):
        raw = raw + pltpu.roll(parts, rows - j * number, 0)
    raw = jnp.where(iota((rows, queries), 0) % tile < number, raw, self_inf)
    out_ref[...] = jnp.zeros_like(out_ref)
    out_ref[:, :queries] = raw


def score(me, number, each, pieces, slots, shares, made, rows_of, high, low):
    block = high.shape[0]
    lanes = pieces[0].shape[2]
    tile = block // lanes * number
    n = sum(map(len, slots))
    queries = n * each
    padded = -(-queries // 128) * 128
    return pl.pallas_call(
        functools.partial(score_kernel, number, each, slots, shares, rows_of),
        out_shape=pltpu.VMEM((n * tile, padded), F32),
        in_specs=[pl.BlockSpec(memory_space=pltpu.SMEM)] + [VMEM] * (len(pieces) + len(made) + 2),
        out_specs=VMEM,
        scratch_shapes=[pltpu.VMEM((n, tile, lanes), F32)],
        compiler_params=pltpu.CompilerParams(vmem_limit_bytes=20 * 2**20),
        name="score",
    )(me, *pieces, *made, high, low)


def finish_kernel(number, parts_ref, out_ref):
    total = jnp.sum(parts_ref[...], axis=0)
    queries = out_ref.shape[1]
    self_inf = total[number : number + 1, :queries]
    out_ref[...] = total[:number, :queries] / jnp.sqrt(self_inf)


def swap(x, k, n):
    return lax.ppermute(x, "dp", [(i, i ^ k) for i in range(n)])


def fast(n, train_hidden, train_cot, query_hidden, query_cot, proj_in, proj_out, hess_inv):
    number, qlen = train_hidden.shape[0], query_hidden.shape[1]
    tokens = query_hidden.shape[0] * qlen
    queries = n * query_hidden.shape[0]
    planes = n // INNER
    me = lax.axis_index("dp").astype(jnp.int32).reshape(1)
    messages = project(
        me, planes, train_hidden, train_cot, query_hidden, query_cot, proj_in, proj_out
    )
    coords = hess_inv.shape[1]
    others = [(INNER * k) ^ 1 for k in range(1, planes)]
    far = [swap(messages[slot // INNER], slot, n) for slot in others]
    edge = (messages[0].shape[0] - tokens) // 2
    by_plane = [messages[0]] + far
    own = swap(messages[0][edge:], 3, n)
    near = swap(messages[1][edge:], others[0] ^ 3, n)
    by_two = jnp.stack([own, near])
    if planes > 2:
        by_two = jnp.concatenate([by_two, swap(jnp.stack(far[1:])[:, edge:], 3, n)], axis=0)
    by_plane = jnp.stack(by_plane)
    by_plane_one = swap(by_plane[:, :-edge], 1, n)
    high, low = split(hess_inv, by_plane)
    made = prepare(tokens, qlen, coords, [edge], by_plane)
    by_two, high, low, made = lax.optimization_barrier((by_two, high, low, made))
    by_two_one = swap(by_two, 1, n)
    made = [
        made,
        prepare(tokens, qlen, coords, [edge, 0], by_plane_one, by_two),
        prepare(tokens, qlen, coords, [0], by_two_one),
    ]
    slots = [[first ^ slot for slot in [0] + others] for first in (0, 1, 3, 2)]
    rows_of = [slots[0], slots[1] + slots[2], slots[3]]
    pieces = [by_plane, by_plane_one, by_two, by_two_one]
    shares = [(0, False), (0, True), (tokens, False), (tokens, True)]
    each = tokens // qlen
    parts = score(me, number, each, pieces, slots, shares, made, rows_of, high, low)
    parts = parts.reshape(n, -1, parts.shape[1])
    parts = lax.all_to_all(parts, "dp", 0, 0, tiled=True)
    return pl.pallas_call(
        functools.partial(finish_kernel, number),
        out_shape=jax.ShapeDtypeStruct((number, queries), F32),
        in_specs=[VMEM],
        out_specs=VMEM,
        compiler_params=pltpu.CompilerParams(vmem_limit_bytes=4 * 2**20),
        name="finish",
    )(pltpu.with_memory_space_constraint(parts, pltpu.VMEM))


def suits(n, args):
    train_hidden, _, query_hidden, _, proj_in, _, hess_inv = args
    number, qlen = train_hidden.shape[0], query_hidden.shape[1]
    tokens = query_hidden.shape[0] * qlen
    lanes = 2 * proj_in.shape[0]
    block = hess_inv.shape[0]
    planes = n // INNER
    return (
        n % INNER == 0
        and planes > 1
        and planes & (planes - 1) == 0
        and lanes == 128
        and block % lanes == 0
        and block // lanes * number == 8
        and tokens % 16 == 0
        and GROUP == 8 * qlen
        and planes * tokens % GROUP == 0
        and 2 * planes * tokens % (2 * GROUP) == 0
    )


def on_device(n, *args):
    return fast(n, *args) if suits(n, args) else general(*args)


def solution(mesh):
    n = mesh.shape["dp"]
    in_specs = (
        P(("groups", "dp"), None, None),
        P(("groups", "dp"), None, None),
        P(("groups", "dp"), None, None),
        P(("groups", "dp"), None, None),
        P(),
        P(),
        P(("groups", "dp"), None),
    )
    out_specs = P(("groups", "dp"), None)
    return jax.shard_map(
        functools.partial(on_device, n),
        mesh=mesh,
        in_specs=in_specs,
        out_specs=out_specs,
        check_vma=False,
    )
```

```python
import functools

import jax
import jax.numpy as jnp
from jax import lax
from jax.experimental import pallas as pl
from jax.experimental.pallas import tpu as pltpu
from jax.sharding import PartitionSpec as P

F32, BF16 = jnp.float32, jnp.bfloat16
NT = (((1,), (1,)), ((), ()))
VMEM = pl.BlockSpec(memory_space=pltpu.VMEM)
HBM = pl.BlockSpec(memory_space=pltpu.HBM)
INNER = 4
GROUP = 128


def dot(a, b):
    return jnp.dot(a, b, preferred_element_type=F32)


def dot_nt(a, b):
    return lax.dot_general(a, b, NT, preferred_element_type=F32)


def in_hbm(x):
    return pltpu.with_memory_space_constraint(x, pltpu.HBM)


def iota(shape, dim):
    return lax.broadcasted_iota(jnp.int32, shape, dim)


def example_grads(hidden, cotangent, proj_in, proj_out):
    number, length, inner = hidden.shape
    outer_width = cotangent.shape[2]
    rank = proj_in.shape[0]
    inputs = jnp.dot(
        hidden.reshape(number * length, inner), proj_in.T, preferred_element_type=jnp.float32
    ).astype(jnp.bfloat16)
    outputs = jnp.dot(
        cotangent.reshape(number * length, outer_width),
        proj_out.T,
        preferred_element_type=jnp.float32,
    ).astype(jnp.bfloat16)
    inputs = inputs.reshape(number, length, rank)
    outputs = outputs.reshape(number, length, rank)
    summed = jnp.einsum("sto,sti->soi", outputs, inputs, preferred_element_type=jnp.float32) * (
        1.0 / length
    )
    return summed.astype(jnp.bfloat16).reshape(number, rank * rank)


def general(train_hidden, train_cot, query_hidden, query_cot, proj_in, proj_out, hess_inv):
    train_grads = example_grads(train_hidden, train_cot, proj_in, proj_out)
    query_grads = example_grads(query_hidden, query_cot, proj_in, proj_out)
    full_query = lax.all_gather(query_grads, "dp", axis=0, tiled=True).astype(jnp.float32)
    product = jnp.dot(full_query, hess_inv.T, precision=lax.Precision.HIGHEST)
    full_precond = lax.all_gather(product.astype(jnp.bfloat16), "dp", axis=1, tiled=True)
    self_inf = jnp.sum(full_query * full_precond.astype(jnp.float32), axis=1)
    raw = jnp.dot(train_grads, full_precond.T, preferred_element_type=jnp.float32)
    return raw / jnp.sqrt(self_inf)[None, :]


def project_kernel(
    planes, number, length, widths, me_ref, th_ref, tc_ref, qh_ref, qc_ref, pi_ref, po_ref, *rest
):
    outs, (th, tc, qh, qc, pi, po, grads, sems) = rest[:planes], rest[planes:]
    inner = th.shape[1]
    rank = pi.shape[0]
    tokens = th.shape[0]
    queries = qh.shape[0]

    copies = []

    def load(*pairs):
        group = []
        for src, dst in pairs:
            group.append(pltpu.make_async_copy(src, dst, sems.at[sum(map(len, copies)) + len(group)]))
            group[-1].start()
        copies.append(group)

    def arrived():
        for copy in copies.pop(0):
            copy.wait()

    parts = [slice(sum(widths[:c]), sum(widths[: c + 1])) for c in range(len(widths))]
    for c, cols in enumerate(parts):
        load(
            (pi_ref.at[:, cols], pi.at[:, cols]),
            (th_ref.at[:, cols], th.at[:, cols]),
            (qh_ref.at[:, cols], qh.at[:, cols]),
        )
        if c == 0:
            load((po_ref, po), (tc_ref, tc), (qc_ref, qc))

    rows = rank // 2 * number
    t_in = jnp.zeros((tokens, rank), F32)
    q_in = jnp.zeros((queries, rank), F32)
    for c, cols in enumerate(parts):
        arrived()
        step = (cols.stop - cols.start) // 4
        for some in [slice(cols.start + i * step, cols.start + (i + 1) * step) for i in range(4)]:
            t_in += dot_nt(th[:, some], pi[:, some])
            q_in += dot_nt(qh[:, some], pi[:, some])
        if c == 0:
            arrived()
            q_out = dot_nt(qc[...], po[...])
            t_out = dot_nt(po[...], tc[...]).astype(BF16)

    row, col = iota((rows, tokens), 0), iota((rows, tokens), 1)
    own = row % number == col // length
    lefts = []
    for half in range(2):
        pick = iota((rows, rank), 1) == 2 * (iota((rows, rank), 0) // number) + half
        lefts.append(jnp.where(own, dot(pick.astype(BF16), t_out), 0.0).astype(BF16))

    spread = jnp.concatenate([t_in, t_in], axis=1).astype(BF16)
    lane = iota((tokens, 2 * rank), 1)
    total = jnp.zeros((rows, 2 * rank), F32)
    for half in range(2):
        right = jnp.where(lane // rank == half, spread, jnp.zeros_like(spread))
        total += dot(lefts[half], right)
    grads[...] = total * (1.0 / length)
    message = jnp.concatenate([q_in, q_out], axis=1).astype(BF16)

    plane, inner = me_ref[0] // INNER, me_ref[0] % INNER
    tile = rows // planes // INNER
    edge = 2 * tile
    for k in range(planes):
        shares = [
            grads[pl.ds(pl.multiple_of(((plane ^ k) * INNER + (inner ^ j)) * tile, tile), tile), :]
            for j in ((0, 1, 3, 2) if k == 0 else (1, 0, 2, 3))
        ]
        outs[k][:edge, :] = jnp.concatenate(shares[:2], axis=0).astype(BF16)
        outs[k][edge : edge + queries, :] = message
        outs[k][edge + queries :, :] = jnp.concatenate(shares[2:], axis=0).astype(BF16)


def project(me, planes, train_hidden, train_cot, query_hidden, query_cot, proj_in, proj_out):
    number, length, inner = train_hidden.shape
    width = train_cot.shape[2]
    rank = proj_in.shape[0]
    tokens, queries = number * length, query_hidden.shape[0] * query_hidden.shape[1]
    rows = rank // 2 * number
    widths = [2048, 4096, 4096, 4096]
    return pl.pallas_call(
        functools.partial(project_kernel, planes, number, length, widths),
        out_shape=[pltpu.VMEM((queries + rows // planes, 2 * rank), BF16)] * planes,
        in_specs=[pl.BlockSpec(memory_space=pltpu.SMEM)] + [HBM] * 6,
        out_specs=[VMEM] * planes,
        scratch_shapes=[
            pltpu.VMEM((tokens, inner), BF16),
            pltpu.VMEM((tokens, width), BF16),
            pltpu.VMEM((queries, inner), BF16),
            pltpu.VMEM((queries, width), BF16),
            pltpu.VMEM((rank, inner), BF16),
            pltpu.VMEM((rank, width), BF16),
            pltpu.VMEM((rows, 2 * rank), F32),
            pltpu.SemaphoreType.DMA((3 * len(widths) + 3,)),
        ],
        compiler_params=pltpu.CompilerParams(vmem_limit_bytes=20 * 2**20),
        name="project",
    )(
        me,
        in_hbm(train_hidden.reshape(tokens, inner)),
        in_hbm(train_cot.reshape(tokens, width)),
        in_hbm(query_hidden.reshape(queries, inner)),
        in_hbm(query_cot.reshape(queries, width)),
        in_hbm(proj_in),
        in_hbm(proj_out),
    )


def build(tok, qlen, grads):
    lanes = tok.shape[1]
    rank = lanes // 2
    pairs = rank // 2
    per = GROUP // qlen
    groups = tok.shape[0] // GROUP
    pick = (iota((rank, lanes), 1) == iota((rank, lanes), 0) + rank).astype(BF16)
    shift = (iota((lanes, lanes), 1) == iota((lanes, lanes), 0) + rank).astype(BF16)
    own = iota((per, GROUP), 1) // qlen == iota((per, GROUP), 0)
    every = tok[...]
    outs = dot_nt(pick, every)
    moved = dot(every, shift).astype(BF16)
    still = jnp.where(iota(every.shape, 1) < rank, every, jnp.zeros_like(every))
    made = []
    for g in range(groups):
        cols = slice(g * GROUP, (g + 1) * GROUP)
        left = [
            jnp.concatenate(
                [
                    jnp.where(own, jnp.broadcast_to(outs[o : o + 1, cols], own.shape), 0.0)
                    for o in range(half, rank, 2)
                ],
                axis=0,
            ).astype(BF16)
            for half in range(2)
        ]
        right = jnp.concatenate([still[cols], moved[cols]], axis=0)
        made.append(dot(jnp.concatenate(left, axis=1), right) * (1.0 / qlen))
    made += [jnp.zeros_like(made[0])] * (groups % 2)
    for g in range(0, groups, 2):
        for pair in range(pairs):
            rows = slice(pair * per, (pair + 1) * per)
            grads[g * per : (g + 2) * per, pair * lanes : (pair + 1) * lanes] = jnp.concatenate(
                [made[g][rows], made[g + 1][rows]], axis=0
            ).astype(BF16)


def split_kernel(chunks, hess_ref, after_ref, high_ref, low_ref, hess, sems):
    width = hess.shape[1] // chunks
    copies = []
    for c in range(chunks):
        cols = pl.ds(c * width, width)
        copies.append(pltpu.make_async_copy(hess_ref.at[:, cols], hess.at[:, cols], sems.at[c]))
        copies[-1].start()
    for c in range(chunks):
        copies[c].wait()
        cols = slice(c * width, (c + 1) * width)
        h = hess[:, cols]
        high = h.astype(BF16)
        high_ref[:, cols] = high
        low_ref[:, cols] = (h - high.astype(F32)).astype(BF16)


def split(hess_inv, after):
    chunks = 4
    return pl.pallas_call(
        functools.partial(split_kernel, chunks),
        out_shape=[pltpu.VMEM(hess_inv.shape, BF16)] * 2,
        in_specs=[HBM, VMEM],
        out_specs=[VMEM] * 2,
        scratch_shapes=[
            pltpu.VMEM(hess_inv.shape, F32),
            pltpu.SemaphoreType.DMA((chunks,)),
        ],
        compiler_params=pltpu.CompilerParams(vmem_limit_bytes=20 * 2**20),
        name="split",
    )(in_hbm(hess_inv), after)


def prepare_kernel(tokens, qlen, starts, *refs):
    pieces, (grads_ref, tok) = refs[:-2], refs[-2:]
    first = 0
    for piece, start in zip(pieces, starts):
        for part in range(piece.shape[0]):
            tok[first : first + tokens, :] = piece[part, start : start + tokens, :]
            first += tokens
    build(tok, qlen, grads_ref)


def prepare(tokens, qlen, coords, starts, *pieces):
    total = sum(piece.shape[0] for piece in pieces) * tokens
    rows = -(-total // (2 * GROUP)) * (2 * GROUP) // qlen
    return pl.pallas_call(
        functools.partial(prepare_kernel, tokens, qlen, starts),
        out_shape=pltpu.VMEM((rows, coords), BF16),
        in_specs=[VMEM] * len(pieces),
        out_specs=VMEM,
        scratch_shapes=[pltpu.VMEM((total, pieces[0].shape[2]), BF16)],
        compiler_params=pltpu.CompilerParams(vmem_limit_bytes=20 * 2**20),
        name="prepare",
    )(*pieces)


def score_kernel(number, each, slots, shares, rows_of, me_ref, *refs):
    pieces, refs = refs[: len(slots)], refs[len(slots) :]
    made_refs, (high_ref, low_ref, out_ref, train) = refs[: len(rows_of)], refs[len(rows_of) :]
    me = me_ref[0]
    block = high_ref.shape[0]
    n, tile, lanes = train.shape
    queries = n * each
    local = block // lanes

    for piece, froms, (first, second) in zip(pieces, slots, shares):
        for part, slot in enumerate(froms):
            both = piece[part, first : first + 2 * tile, :].astype(F32)
            train[me ^ slot] = both[tile:] if second else both[:tile]
    grads = jnp.concatenate([ref[...] for ref in made_refs], axis=0)
    precond = dot_nt(high_ref[...], grads) + dot_nt(low_ref[...], grads)
    row, col = iota((grads.shape[0], queries), 0), iota((grads.shape[0], queries), 1)
    place = jnp.full(row.shape, -1, jnp.int32)
    first = 0
    for ref, froms in zip(made_refs, rows_of):
        for i, slot in enumerate(froms):
            at = row - (first + i * each)
            place = jnp.where((at >= 0) & (at < each), (me ^ slot) * each + at, place)
        first += ref.shape[0]
    order = place == col
    precond = dot(precond.astype(BF16), order.astype(BF16)).astype(BF16)

    cols = pl.ds(pl.multiple_of(me * block, block), block)
    square = dot(jnp.concatenate([ref[:, cols] for ref in made_refs], axis=0), precond)
    self_inf = jnp.sum(jnp.where(order, square, 0.0), axis=0, keepdims=True)

    rows = n * tile
    t = train[...].reshape(rows, lanes)
    where = iota((rows, lanes), 0) % tile // number
    wide = jnp.concatenate(
        [jnp.where(where == j, t, 0.0).astype(BF16) for j in range(local)], axis=1
    )
    parts = dot(wide, precond)
    raw = parts
    for j in range(1, local):
        raw = raw + pltpu.roll(parts, rows - j * number, 0)
    raw = jnp.where(iota((rows, queries), 0) % tile < number, raw, self_inf)
    out_ref[...] = jnp.zeros_like(out_ref)
    out_ref[:, :queries] = raw


def score(me, number, each, pieces, slots, shares, made, rows_of, high, low):
    block = high.shape[0]
    lanes = pieces[0].shape[2]
    tile = block // lanes * number
    n = sum(map(len, slots))
    queries = n * each
    padded = -(-queries // 128) * 128
    return pl.pallas_call(
        functools.partial(score_kernel, number, each, slots, shares, rows_of),
        out_shape=pltpu.VMEM((n * tile, padded), F32),
        in_specs=[pl.BlockSpec(memory_space=pltpu.SMEM)] + [VMEM] * (len(pieces) + len(made) + 2),
        out_specs=VMEM,
        scratch_shapes=[pltpu.VMEM((n, tile, lanes), F32)],
        compiler_params=pltpu.CompilerParams(vmem_limit_bytes=20 * 2**20),
        name="score",
    )(me, *pieces, *made, high, low)


def finish_kernel(number, parts_ref, out_ref):
    total = jnp.sum(parts_ref[...], axis=0)
    queries = out_ref.shape[1]
    self_inf = total[number : number + 1, :queries]
    out_ref[...] = total[:number, :queries] / jnp.sqrt(self_inf)


def swap(x, k, n):
    return lax.ppermute(x, "dp", [(i, i ^ k) for i in range(n)])


def fast(n, train_hidden, train_cot, query_hidden, query_cot, proj_in, proj_out, hess_inv):
    number, qlen = train_hidden.shape[0], query_hidden.shape[1]
    tokens = query_hidden.shape[0] * qlen
    queries = n * query_hidden.shape[0]
    planes = n // INNER
    me = lax.axis_index("dp").astype(jnp.int32).reshape(1)
    messages = project(
        me, planes, train_hidden, train_cot, query_hidden, query_cot, proj_in, proj_out
    )
    coords = hess_inv.shape[1]
    others = [(INNER * k) ^ 1 for k in [1] + list(range(planes - 1, 1, -1))]
    far = [swap(messages[slot // INNER], slot, n) for slot in others]
    edge = (messages[0].shape[0] - tokens) // 2
    by_plane = [messages[0]] + far
    own = swap(messages[0][edge:], 3, n)
    near = swap(messages[1][edge:], others[0] ^ 3, n)
    by_two = jnp.stack([own, near])
    if planes > 2:
        by_two = jnp.concatenate([by_two, swap(jnp.stack(far[1:])[:, edge:], 3, n)], axis=0)
    by_plane = jnp.stack(by_plane)
    by_plane_one = swap(by_plane[:, :-edge], 1, n)
    high, low = split(hess_inv, by_plane)
    made = prepare(tokens, qlen, coords, [edge], by_plane)
    by_two, high, low, made = lax.optimization_barrier((by_two, high, low, made))
    by_two_one = swap(by_two, 1, n)
    made = [
        made,
        prepare(tokens, qlen, coords, [edge, 0], by_plane_one, by_two),
        prepare(tokens, qlen, coords, [0], by_two_one),
    ]
    slots = [[first ^ slot for slot in [0] + others] for first in (0, 1, 3, 2)]
    rows_of = [slots[0], slots[1] + slots[2], slots[3]]
    pieces = [by_plane, by_plane_one, by_two, by_two_one]
    shares = [(0, False), (0, True), (tokens, False), (tokens, True)]
    each = tokens // qlen
    parts = score(me, number, each, pieces, slots, shares, made, rows_of, high, low)
    parts = parts.reshape(n, -1, parts.shape[1])
    parts = lax.all_to_all(parts, "dp", 0, 0, tiled=True)
    return pl.pallas_call(
        functools.partial(finish_kernel, number),
        out_shape=jax.ShapeDtypeStruct((number, queries), F32),
        in_specs=[VMEM],
        out_specs=VMEM,
        compiler_params=pltpu.CompilerParams(vmem_limit_bytes=4 * 2**20),
        name="finish",
    )(pltpu.with_memory_space_constraint(parts, pltpu.VMEM))


def suits(n, args):
    train_hidden, _, query_hidden, _, proj_in, _, hess_inv = args
    number, qlen = train_hidden.shape[0], query_hidden.shape[1]
    tokens = query_hidden.shape[0] * qlen
    lanes = 2 * proj_in.shape[0]
    block = hess_inv.shape[0]
    planes = n // INNER
    return (
        n % INNER == 0
        and planes > 1
        and planes & (planes - 1) == 0
        and lanes == 128
        and block % lanes == 0
        and block // lanes * number == 8
        and tokens % 16 == 0
        and GROUP == 8 * qlen
        and planes * tokens % GROUP == 0
        and 2 * planes * tokens % (2 * GROUP) == 0
    )


def on_device(n, *args):
    return fast(n, *args) if suits(n, args) else general(*args)


def solution(mesh):
    n = mesh.shape["dp"]
    in_specs = (
        P(("groups", "dp"), None, None),
        P(("groups", "dp"), None, None),
        P(("groups", "dp"), None, None),
        P(("groups", "dp"), None, None),
        P(),
        P(),
        P(("groups", "dp"), None),
    )
    out_specs = P(("groups", "dp"), None)
    return jax.shard_map(
        functools.partial(on_device, n),
        mesh=mesh,
        in_specs=in_specs,
        out_specs=out_specs,
        check_vma=False,
    )
```
